256 devices in a mesh: expert: 64 (over x, z, core), dp: 4 (over y).
Axes of the slice: x: 4, y: 4, z: 8, core: 2. Of those that a mesh axis runs over, the one named last changes fastest.
Arguments:
- tokens: bfloat16 [32768, 2048], P(('expert', 'dp')), may hold values from -6 to 6
- cotangent: bfloat16 [32768, 2048], P(('expert', 'dp')), may hold values from -6 to 6
- w_in: bfloat16 [64, 2048, 2048], P('expert', None, 'dp'), may hold values from -0.125 to 0.125
- w_out: bfloat16 [64, 2048, 2048], P('expert', 'dp'), may hold values from -0.125 to 0.125
- expert_tokens: int32 [64, 512], replicated, may hold values from 0 to 32767, as said below
- gate_weights: float32 [64, 512], P('expert'), may hold values from 0.2 to 1
Outputs:
- grad_tokens: bfloat16 [32768, 2048], P(('expert', 'dp'))
- grad_w_in: bfloat16 [64, 2048, 2048], P('expert', None, 'dp')
- grad_w_out: bfloat16 [64, 2048, 2048], P('expert', 'dp')
- grad_gates: float32 [64, 512], P('expert')
The draws below stay inside these ranges and needn't reach their ends.
Inputs may be any that keep to these rules, and one draw needn't show every extreme that they name: `expert_tokens`: each row holds 512 distinct token ids. Counting the tokens of a device as the 128 consecutive ids id // 128, each expert takes at most 4 tokens from one device, and exactly 4 from at least one device.
All inputs are finite; a program needn't handle non-finite values.
Results may differ from the reference program's by a relative error of at most 0.015.
Values may be sent and summed in bfloat16 or wider, within the bound.
No kernel may reach another device: no remote copies, remote signals or barrier semaphores. Data moves between devices by JAX's collectives and lax.ppermute only.
A program may use at most 128 MiB of HBM per device.

```python
import jax
import jax.numpy as jnp
from jax import lax

D = 2048
FF = 2048
TOK_DEV = 128
EXPERTS = 64
OWNERS = 256
TOKENS = 32768
CAP = 512
MOST = 4
N_DP = 4


def draw_expert_tokens(key, part):
    key = jax.random.fold_in(key, 11)

    def one_expert(expert_num):
        sub_key = jax.random.fold_in(key, expert_num)
        key_local, key_order, key_full, key_final = jax.random.split(sub_key, 4)
        owner_keys = jax.random.split(key_local, OWNERS)
        local_pick = jax.vmap(lambda owner_key: jax.random.permutation(owner_key, TOK_DEV)[:MOST])(owner_keys)
        candidates = (jnp.arange(OWNERS, dtype=jnp.int32)[:, None] * TOK_DEV + local_pick.astype(jnp.int32)).reshape(-1)
        order = jax.random.permutation(key_order, OWNERS * MOST).astype(jnp.int32)
        full_owner = jax.random.randint(key_full, (), 0, OWNERS)
        owner_of = jnp.arange(OWNERS * MOST, dtype=jnp.int32) // MOST
        scores = jnp.where(owner_of == full_owner, -1, order)
        picked = candidates[jnp.argsort(scores, stable=True)[:CAP]]
        return picked[jax.random.permutation(key_final, CAP)]
    return lax.map(one_expert, jnp.arange(EXPERTS, dtype=jnp.int32)).astype(jnp.int32)


def block_scale(key, dims, shards, low, top_value):
    level = 1.0
    for dim, blocks in shards:
        steps = jax.random.uniform(jax.random.fold_in(jax.random.fold_in(key, 6), dim), (blocks,), jnp.float32, low / len(shards), top_value / len(shards))
        level = level * jnp.repeat(jnp.exp(steps), dims[dim] // blocks).reshape((-1,) + (1,) * (len(dims) - 1 - dim))
    return level


def centred(key, shape, deviation, limit, cuts=(), kind=jnp.bfloat16):
    array = jax.random.normal(key, shape, jnp.float32) * deviation
    if len(cuts) > 0:
        array = block_scale(key, shape, cuts, -0.22, 0.18) * array
    return jnp.clip(array, min=-limit, max=limit).astype(kind)


def setup_inputs(seed: int = 0) -> dict:
    key_of = jax.random.split(jax.random.key(seed), 7)
    tokens = centred(key_of[0], (TOKENS, D), 1.0, 6.0, ((0, 256),))
    cotangent = centred(key_of[1], (TOKENS, D), 1.0, 6.0, ((0, 256),))
    w_in = centred(key_of[2], (EXPERTS, D, FF), D ** -0.5, 0.125, ((0, 64), (2, 4)))
    w_out = centred(key_of[3], (EXPERTS, FF, D), FF ** -0.5, 0.125, ((0, 64), (1, 4)))
    expert_tokens = draw_expert_tokens(jax.random.fold_in(key_of[6], 71), 0)
    gate_weights = jnp.clip(0.2 + 0.8 * jax.random.uniform(key_of[5], (EXPERTS, CAP), jnp.float32) ** block_scale(key_of[5], (EXPERTS, CAP), ((0, 64),), -0.2, 0.2), 0.2, 1.0)
    return {"tokens": tokens, "cotangent": cotangent, "w_in": w_in, "w_out": w_out, "expert_tokens": expert_tokens, "gate_weights": gate_weights}


GELU_SCALE = 0.7978845608028654
GELU_CUBIC = 0.044715


def gelu_pair(pre_act):
    inner_arg = GELU_SCALE * (pre_act + GELU_CUBIC * pre_act * pre_act * pre_act)
    tanh_val = jnp.tanh(inner_arg)
    gelu_value = 0.5 * pre_act * (1.0 + tanh_val)
    gelu_slope = 0.5 * (1.0 + tanh_val) + 0.5 * pre_act * (1.0 - tanh_val * tanh_val) * GELU_SCALE * (1.0 + 3.0 * GELU_CUBIC * pre_act * pre_act)
    return gelu_value, gelu_slope


def reference(tokens, cotangent, w_in, w_out, expert_tokens, gate_weights):
    block_ff = FF // N_DP

    def per_expert(carry, packed):
        w_in_one, w_out_one, ids_one, gate_one = packed
        rows_in = tokens[ids_one]
        rows_cot = cotangent[ids_one]
        pre_act = jnp.dot(rows_in, w_in_one, preferred_element_type=jnp.float32)
        gelu_value, gelu_slope = gelu_pair(pre_act)
        hidden = gelu_value.astype(jnp.bfloat16)
        full_out = jnp.dot(hidden, w_out_one, preferred_element_type=jnp.float32)
        grad_gate = jnp.sum(rows_cot.astype(jnp.float32) * full_out, axis=1)
        scaled = (gate_one[:, None] * rows_cot.astype(jnp.float32)).astype(jnp.bfloat16)
        grad_w_out = jnp.dot(hidden.T, scaled, preferred_element_type=jnp.float32).astype(jnp.bfloat16)
        grad_hidden = jnp.dot(scaled, w_out_one.T, preferred_element_type=jnp.float32)
        grad_pre = (grad_hidden * gelu_slope).astype(jnp.bfloat16)
        grad_w_in = jnp.dot(rows_in.T, grad_pre, preferred_element_type=jnp.float32).astype(jnp.bfloat16)
        summed = jnp.zeros((CAP, D), jnp.float32)
        for quarter in range(N_DP):
            lower = quarter * block_ff
            piece = jnp.dot(grad_pre[:, lower:lower + block_ff], w_in_one[:, lower:lower + block_ff].T, preferred_element_type=jnp.float32)
            summed = summed + lax.optimization_barrier(piece.astype(jnp.bfloat16)).astype(jnp.float32)
        row_grads = lax.optimization_barrier(summed.astype(jnp.bfloat16)).astype(jnp.float32)
        carry = carry.at[ids_one].add(row_grads)
        return carry, (grad_w_in, grad_w_out, grad_gate)

    start = jnp.zeros((TOKENS, D), jnp.float32)
    total, stacked = lax.scan(per_expert, start, (w_in, w_out, expert_tokens, gate_weights))
    return total.astype(jnp.bfloat16), stacked[0], stacked[1], stacked[2]
```

```python
import functools

import jax
import jax.numpy as jnp
from jax import lax
from jax.experimental import pallas as pl
from jax.experimental.pallas import tpu as pltpu
from jax.sharding import PartitionSpec as P

GELU_SCALE = 0.7978845608028654
GELU_CUBIC = 0.044715
MOST = 4
BF16 = jnp.bfloat16
F32 = jnp.float32
VMEM = pl.BlockSpec(memory_space=pltpu.VMEM)
SMEM = pl.BlockSpec(memory_space=pltpu.SMEM)
PARAMS = pltpu.CompilerParams(vmem_limit_bytes=48 * 1024 * 1024)
OFFSETS = (0, -1, 1, 2)


def gelu_pair(pre_act):
    inner_arg = GELU_SCALE * (pre_act + GELU_CUBIC * pre_act * pre_act * pre_act)
    tanh_val = jnp.tanh(inner_arg)
    gelu_value = 0.5 * pre_act * (1.0 + tanh_val)
    gelu_slope = 0.5 * (1.0 + tanh_val) + 0.5 * pre_act * (
        1.0 - tanh_val * tanh_val
    ) * GELU_SCALE * (1.0 + 3.0 * GELU_CUBIC * pre_act * pre_act)
    return (gelu_value, gelu_slope)


def dot(a, b, da=1, db=0):
    return lax.dot_general(a, b, (((da,), (db,)), ((), ())), preferred_element_type=F32)


def iota(shape, dim):
    return lax.broadcasted_iota(jnp.int32, shape, dim)


def ones_where(mask):
    return jnp.where(mask, 1.0, 0.0).astype(BF16)


def call(kernel, outs, *args, flops=0, smem=0):
    moved = sum(a.size * a.dtype.itemsize for a in (*args, *outs))
    return pl.pallas_call(
        kernel,
        out_shape=tuple(outs),
        in_specs=[SMEM] * smem + [VMEM] * (len(args) - smem),
        out_specs=tuple(VMEM for _ in outs),
        compiler_params=PARAMS,
        cost_estimate=pl.CostEstimate(flops=flops, bytes_accessed=moved, transcendentals=0),
    )(*args)


def shape_of(*dims, dtype=BF16):
    return jax.ShapeDtypeStruct(dims, dtype)


def running_count(mask):
    width = mask.shape[1]
    upper = ones_where(iota((width, width), 0) <= iota((width, width), 1))
    return dot(ones_where(mask), upper)


def send_kernel(place, ids, tokens, cotangent, out_tok, out_cot, picker, most):
    experts, _ = ids.shape
    tok_dev, width = tokens.shape
    half = width // 2
    rows = experts * MOST * 2
    id_all = ids[...]
    owner = id_all // tok_dev
    local = id_all - owner * tok_dev
    mine = owner == place[0]
    rank = running_count(mine)
    lane = iota((experts, 128), 1)
    wanted = jnp.zeros((experts, 128), F32)
    for level in range(MOST):
        hit = mine & (rank == level + 1.0)
        found = jnp.sum(jnp.where(hit, local + 1, 0).astype(F32), axis=1, keepdims=True)
        wanted = jnp.where(lane == level, found, wanted)
    spread = ones_where(iota((rows, experts), 0) // (2 * MOST) == iota((rows, experts), 1))
    by_row = dot(spread, wanted.astype(BF16))
    row_level = iota((rows, 128), 0) % (2 * MOST) // 2
    want = jnp.sum(jnp.where(row_level == iota((rows, 128), 1), by_row, 0.0), axis=1, keepdims=True)
    column = iota((rows, 2 * tok_dev), 1)
    side = iota((rows, 2 * tok_dev), 0) % 2
    pick = ones_where(
        (column // tok_dev == side) & ((column % tok_dev + 1).astype(F32) == want)
    )
    picker[...] = pick
    for source, out in ((tokens, out_tok), (cotangent, out_cot)):
        stacked = jnp.concatenate([source[:, :half], source[:, half:]], axis=0)
        out[...] = dot(pick, stacked).astype(BF16)
    plane = owner % 4
    fullest = jnp.zeros((), F32)
    for dp in range(4):
        held = jnp.sum(jnp.where(plane == dp, 1.0, 0.0), axis=1, keepdims=True)
        fullest = jnp.maximum(fullest, jnp.max(held))
    most[...] = jnp.full((8, 128), fullest.astype(jnp.int32), jnp.int32)


def index_kernel(place, ids, gates, row_slot, row_gate, pack, unpack, *, cap, tok_dev):
    slots = ids.shape[1]
    experts = pack.shape[1] // (2 * MOST)
    my_dp = place[1]
    owner = ids[...] // tok_dev
    plane = owner % 4
    block = iota((8, slots), 0)
    wanted_plane = jnp.zeros((8, slots), jnp.int32)
    for j, offset in enumerate(OFFSETS):
        wanted_plane = jnp.where(block == j, (my_dp + offset + 4) % 4, wanted_plane)
    on_plane = (wanted_plane == plane) & (block < 4)
    position = running_count(on_plane)
    gate = gates[...]
    first = None
    for j in range(4):
        at = iota((cap, slots), 0).astype(F32) + 1.0
        hit = (position[j : j + 1, :] == at) & on_plane[j : j + 1, :]
        hot = ones_where(hit)
        row_slot[j * cap : (j + 1) * cap, :] = hot
        row_gate[j * cap : (j + 1) * cap, :] = jnp.sum(
            jnp.where(hit, gate, 0.0), axis=1, keepdims=True
        )
        if first is None:
            first = hot
    from_owner = owner == iota((experts, slots), 0) * 4 + my_dp
    count = running_count(from_owner)
    rank = jnp.sum(jnp.where(from_owner, count, 0.0), axis=0, keepdims=True)
    rows = experts * MOST * 2
    row = iota((rows, slots), 0)
    landing = ones_where(
        (owner == row // (2 * MOST) * 4 + my_dp)
        & (rank == (row % (2 * MOST) // 2 + 1).astype(F32))
    )
    pack[...] = dot(first, landing, 1, 1).astype(BF16)
    unpack[...] = dot(landing, first, 1, 1).astype(BF16)


def pack_kernel(pack, landed, *outs):
    matrix = pack[...]
    side = iota(matrix.shape, 1) % 2
    rows = landed[...]
    for half, out in enumerate(outs):
        out[...] = dot(jnp.where(side == half, matrix, jnp.zeros_like(matrix)), rows).astype(BF16)


def hidden_kernel(w_in, *refs):
    parts, (hidden, slope) = refs[:8], refs[8:]
    cap, half = parts[0].shape
    for j in range(4):
        pre_act = dot(parts[2 * j][...], w_in[:half, :]) + dot(parts[2 * j + 1][...], w_in[half:, :])
        value, grad = gelu_pair(pre_act)
        hidden[j * cap : (j + 1) * cap, :] = value.astype(BF16)
        slope[j * cap : (j + 1) * cap, :] = grad


def grad_kernel(w_in, w_out, hidden, slope, row_gate, row_slot, *refs):
    parts, (grad_pre, gate_part, *pieces) = refs[:8], refs[8:]
    cap, half = parts[0].shape
    total = jnp.zeros(gate_part.shape, F32)
    for j in range(4):
        here = slice(j * cap, (j + 1) * cap)
        grad_out = dot(parts[2 * j][...], w_out[:, :half], 1, 1) + dot(
            parts[2 * j + 1][...], w_out[:, half:], 1, 1
        )
        per_row = jnp.sum(hidden[here, :].astype(F32) * grad_out, axis=1, keepdims=True)
        total += jnp.sum(
            jnp.where(row_slot[here, :] > 0, per_row, 0.0), axis=0, keepdims=True
        )
        pre = (grad_out * row_gate[here, :] * slope[here, :]).astype(BF16)
        grad_pre[here, :] = pre
        pieces[j][...] = dot(pre, w_in[...], 1, 1).astype(BF16)
    gate_part[...] = total


def weight_kernel(hidden, row_gate, grad_pre, *refs):
    toks, cots, (grad_in, grad_out) = refs[:8], refs[8:16], refs[16:]
    cap, half = toks[0].shape
    gated = (hidden[...].astype(F32) * row_gate[...]).astype(BF16)
    for side in range(2):
        here = slice(side * half, (side + 1) * half)
        cot = jnp.concatenate([cots[2 * j + side][...] for j in range(4)], axis=0)
        grad_out[:, here] = dot(gated, cot, 0, 0).astype(BF16)
        tok = jnp.concatenate([toks[2 * j + side][...] for j in range(4)], axis=0)
        grad_in[here, :] = dot(tok, grad_pre[...], 0, 0).astype(BF16)


def unpack_kernel(unpack, one, two, three, four, out):
    matrix = unpack[...]
    half = out.shape[1]
    side = iota(matrix.shape, 0) % 2
    total = jnp.zeros(out.shape, F32)
    for part in range(2):
        here = slice(part * half, (part + 1) * half)
        summed = (
            one[:, here].astype(F32) + two[:, here].astype(F32) + three[:, here].astype(F32) + four[:, here].astype(F32)
        ).astype(BF16)
        total += dot(jnp.where(side == part, matrix, jnp.zeros_like(matrix)), summed)
    out[...] = total.astype(BF16)


def token_kernel(picker, landed, out):
    tok_dev, width = out.shape
    half = width // 2
    for side in range(2):
        out[:, side * half : (side + 1) * half] = dot(
            picker[:, side * tok_dev : (side + 1) * tok_dev], landed[...], 0, 0
        ).astype(BF16)


def shift(array, step):
    return lax.ppermute(array, "dp", [(d, (d + step) % 4) for d in range(4)])


def spread_rows(one, two):
    left_one = shift(one, 1)
    right_two = shift(two, -1)
    left_two = shift(two, 1)
    right_one = shift(one, -1)
    far_one = shift(left_one, 1)
    far_two = shift(right_two, -1)
    return (one, two, left_one, left_two, right_one, right_two, far_one, far_two)


def exchange(array):
    return lax.all_to_all(array, "expert", split_axis=0, concat_axis=0, tiled=True)


def rest(cap, place, my_ids, gate, w_in, w_out, picker, out_tok, out_cot):
    width, units = w_in.shape
    rows = out_tok.shape[0]
    half = width // 2
    slots = my_ids.shape[1]
    tok_dev = picker.shape[1] // 2
    row_slot, row_gate, pack, unpack = call(
        functools.partial(index_kernel, cap=cap, tok_dev=tok_dev),
        [shape_of(4 * cap, slots), shape_of(4 * cap, 1, dtype=F32), shape_of(cap, rows), shape_of(rows, cap)],
        place, my_ids, gate, smem=1, flops=4 * cap * rows * slots,
    )
    half_row = shape_of(cap, half)
    land_tok = exchange(out_tok)
    toks = spread_rows(*call(pack_kernel, [half_row] * 2, pack, land_tok, flops=4 * cap * rows * half))
    land_cot = exchange(out_cot)
    cots = spread_rows(*call(pack_kernel, [half_row] * 2, pack, land_cot, flops=4 * cap * rows * half))
    product = 2 * 4 * cap * width * units
    hidden, slope = call(
        hidden_kernel,
        [shape_of(4 * cap, units), shape_of(4 * cap, units, dtype=F32)],
        w_in, *toks, flops=product,
    )
    grad_pre, gate_part, own, left, right, far = call(
        grad_kernel,
        [shape_of(4 * cap, units), shape_of(1, slots, dtype=F32)] + [shape_of(cap, width)] * 4,
        w_in, w_out, hidden, slope, row_gate, row_slot, *cots, flops=2 * product,
    )
    from_left = shift(right, 1)
    from_right = shift(left, -1)
    from_far = shift(far, 2)
    gate_far = shift(gate_part, 2)
    gate_left = shift(gate_part, 1)
    gate_right = shift(gate_part, -1)
    grad_w_in, grad_w_out = call(
        weight_kernel,
        [shape_of(width, units), shape_of(units, width)],
        hidden, row_gate, grad_pre, *toks, *cots, flops=2 * product,
    )
    back = call(
        unpack_kernel, [shape_of(rows, half)], unpack, own, from_left, from_right, from_far, flops=4 * cap * rows * half
    )[0]
    merged = exchange(back)
    grad_tokens = call(token_kernel, [shape_of(tok_dev, width)], picker, merged, flops=2 * tok_dev * rows * width)[0]
    grad_gates = (gate_part + gate_far) + (gate_left + gate_right)
    return (grad_tokens, grad_w_in[None], grad_w_out[None], grad_gates)


def body(tokens, cotangent, w_in, w_out, expert_tokens, gate_weights):
    tok_dev, width = tokens.shape
    experts, slots = expert_tokens.shape
    expert_idx = lax.axis_index("expert")
    dp_idx = lax.axis_index("dp")
    place = jnp.stack([expert_idx * 4 + dp_idx, dp_idx]).astype(jnp.int32)
    rows = experts * MOST * 2
    out_tok, out_cot, picker, most = call(
        send_kernel,
        [shape_of(rows, width // 2)] * 2 + [shape_of(rows, 2 * tok_dev), shape_of(8, 128, dtype=jnp.int32)],
        place, expert_tokens, tokens, cotangent, smem=1, flops=4 * rows * tok_dev * width * 2,
    )
    my_ids = lax.dynamic_slice_in_dim(expert_tokens, expert_idx, 1, 0)
    args = (place, my_ids, gate_weights, w_in[0], w_out[0], picker, out_tok, out_cot)
    full = experts * MOST
    small = SMALL
    if small >= full:
        return rest(full, *args)
    return lax.cond(
        most[0, 0] <= small, functools.partial(rest, small), functools.partial(rest, full), *args
    )


SMALL = 160


def solution(mesh):
    placed = (
        P(("expert", "dp"), None),
        P(("expert", "dp"), None),
        P("expert", None, "dp"),
        P("expert", "dp", None),
        P(),
        P("expert", None),
    )
    return jax.shard_map(
        body,
        mesh=mesh,
        in_specs=placed,
        out_specs=(
            P(("expert", "dp"), None),
            P("expert", None, "dp"),
            P("expert", "dp", None),
            P("expert", None),
        ),
        check_vma=False,
    )
```

```python
import functools

import jax
import jax.numpy as jnp
from jax import lax
from jax.experimental import pallas as pl
from jax.experimental.pallas import tpu as pltpu
from jax.sharding import PartitionSpec as P

GELU_SCALE = 0.7978845608028654
GELU_CUBIC = 0.044715
MOST = 4
BF16 = jnp.bfloat16
F32 = jnp.float32
VMEM = pl.BlockSpec(memory_space=pltpu.VMEM)
SMEM = pl.BlockSpec(memory_space=pltpu.SMEM)
HBM = pl.BlockSpec(memory_space=pltpu.HBM)
OFFSETS = (0, -1, 1, 2)
SMALL = 48


def gelu_pair(pre_act):
    inner_arg = GELU_SCALE * (pre_act + GELU_CUBIC * pre_act * pre_act * pre_act)
    tanh_val = jnp.tanh(inner_arg)
    gelu_value = 0.5 * pre_act * (1.0 + tanh_val)
    gelu_slope = 0.5 * (1.0 + tanh_val) + 0.5 * pre_act * (
        1.0 - tanh_val * tanh_val
    ) * GELU_SCALE * (1.0 + 3.0 * GELU_CUBIC * pre_act * pre_act)
    return (gelu_value, gelu_slope)


def dot(a, b, da=1, db=0):
    return lax.dot_general(a, b, (((da,), (db,)), ((), ())), preferred_element_type=F32)


def iota(shape, dim):
    return lax.broadcasted_iota(jnp.int32, shape, dim)


def ones_where(mask):
    return jnp.where(mask, 1.0, 0.0).astype(BF16)


def keep(mask, array):
    return jnp.where(mask, array, jnp.zeros_like(array))


def call(kernel, outs, *args, flops=0, smem=0, far=0, scratch=(), mib=16):
    moved = sum(a.size * a.dtype.itemsize for a in (*args, *outs))
    return pl.pallas_call(
        kernel,
        out_shape=tuple(outs),
        in_specs=[SMEM] * smem + [VMEM] * (len(args) - smem - far) + [HBM] * far,
        out_specs=tuple(VMEM for _ in outs),
        scratch_shapes=list(scratch),
        compiler_params=pltpu.CompilerParams(vmem_limit_bytes=mib * 1024 * 1024),
        cost_estimate=pl.CostEstimate(flops=flops, bytes_accessed=moved, transcendentals=0),
    )(*args)


def shape_of(*dims, dtype=BF16):
    return jax.ShapeDtypeStruct(dims, dtype)


def running_count(mask):
    width = mask.shape[1]
    upper = ones_where(iota((width, width), 0) <= iota((width, width), 1))
    return dot(ones_where(mask), upper)


def send_kernel(place, ids, tokens, cotangent, first, second, picker, stacked, sems):
    experts, _ = ids.shape
    tok_dev, width = tokens.shape
    half = width // 2
    rows = experts * 8
    copies = []
    for q in range(4):
        source = (tokens, cotangent)[q // 2]
        copies.append(
            pltpu.make_async_copy(
                source.at[:, pl.ds(q % 2 * half, half)],
                stacked.at[pl.ds(q * tok_dev, tok_dev), :],
                sems.at[q],
            )
        )
        copies[-1].start()
    id_all = ids[...]
    owner = id_all // tok_dev
    local = id_all - owner * tok_dev
    mine = owner == place[0]
    rank = running_count(mine)
    lane = iota((experts, 128), 1)
    wanted = jnp.zeros((experts, 128), F32)
    for level in range(MOST):
        hit = mine & (rank == level + 1.0)
        found = jnp.sum(jnp.where(hit, local + 1, 0).astype(F32), axis=1, keepdims=True)
        wanted = jnp.where(lane == level, found, wanted)
    spread = ones_where(iota((rows, experts), 0) // 8 == iota((rows, experts), 1))
    by_row = dot(spread, wanted.astype(BF16))
    row = iota((rows, 128), 0) % 8
    lanes = iota((rows, 128), 1)

    def pick(level, part, parts):
        want = jnp.sum(jnp.where(level == lanes, by_row, 0.0), axis=1, keepdims=True)
        column = iota((rows, parts * tok_dev), 1)
        here = iota((rows, parts * tok_dev), 0) % 8
        return ones_where(
            (column // tok_dev == part(here)) & ((column % tok_dev + 1).astype(F32) == want)
        )

    one = pick(row // 4, lambda r: r % 4, 4)
    two = pick(row // 4 + 2, lambda r: r % 4, 4)
    picker[...] = pick(row // 2, lambda r: r % 2, 2)
    for copy in copies:
        copy.wait()
    first[...] = dot(one, stacked[...]).astype(BF16)
    second[...] = dot(two, stacked[...]).astype(BF16)


def index_kernel(place, ids, gates, everyone, row_slot, row_gate, pack, unpack, most, *, cap, tok_dev):
    slots = ids.shape[1]
    rows = unpack.shape[0]
    experts = rows // 8
    early = 2 * experts
    my_dp = place[1]
    owner = ids[...] // tok_dev
    plane = owner % 4
    gate = gates[...]
    rank = jnp.zeros((1, slots), F32)
    for dp in range(4):
        from_owner = owner == iota((experts, slots), 0) * 4 + dp
        count = running_count(from_owner)
        rank += jnp.sum(jnp.where(from_owner, count, 0.0), axis=0, keepdims=True)
    block = iota((8, slots), 0)
    plane_of = jnp.zeros((8, slots), jnp.int32)
    for j, offset in enumerate(OFFSETS):
        plane_of = jnp.where(block == j, (my_dp + offset + 4) % 4, plane_of)
    late = (plane_of == plane) & (block < 4) & (rank > 2.5)
    position = running_count(late)
    row_a = iota((early, slots), 0)
    row_b = iota((cap, slots), 0).astype(F32) + 1.0
    for j, offset in enumerate(OFFSETS):
        there = (my_dp + offset + 4) % 4
        at = j * (early + cap)
        hit = (owner == row_a // 2 * 4 + there) & (rank == (row_a % 2 + 1).astype(F32))
        here = slice(at, at + early)
        row_slot[here, :] = ones_where(hit)
        row_gate[here, :] = jnp.sum(jnp.where(hit, gate, 0.0), axis=1, keepdims=True)
        hit = (position[j : j + 1, :] == row_b) & late[j : j + 1, :]
        here = slice(at + early, at + early + cap)
        row_slot[here, :] = ones_where(hit)
        row_gate[here, :] = jnp.sum(jnp.where(hit, gate, 0.0), axis=1, keepdims=True)
    row = iota((rows, slots), 0)
    on_row = owner == row // 8 * 4 + my_dp
    arrived = ones_where(on_row & (rank == (row % 8 // 4 + 3).astype(F32)))
    pack[...] = dot(row_slot[early : early + cap, :], arrived, 1, 1).astype(BF16)
    leaving = ones_where(on_row & (rank == (row % 8 // 2 + 1).astype(F32)))
    unpack[...] = dot(leaving, row_slot[: early + cap, :], 1, 1).astype(BF16)
    most[...] = jnp.broadcast_to(fullest(everyone, tok_dev), most.shape).astype(jnp.int32)


def order_kernel(landed, tok, cot):
    count = tok.shape[0]
    shape = (count, landed.shape[0])
    half = landed.shape[1]
    column = iota(shape, 1)
    level = iota(shape, 0) == column // 4
    for q in range(4):
        out = (tok, cot)[q // 2]
        out[:, q % 2 * half : (q % 2 + 1) * half] = dot(
            ones_where(level & (column % 4 == q)), landed[...]
        ).astype(BF16)


def pack_kernel(pack, landed, both):
    matrix = pack[...]
    half = landed.shape[1]
    quarter = iota(matrix.shape, 1) % 4
    for q in range(4):
        both[:, q * half : (q + 1) * half] = dot(keep(quarter == q, matrix), landed[...]).astype(BF16)


def stack(early, late, at, step):
    here = slice(at, at + step)
    return jnp.concatenate([part[:, here] for pair in zip(early, late) for part in pair], axis=0)


def hidden_kernel(w_in, *refs):
    parts, (hidden, slope) = refs[:4], refs[4:]
    value, grad = gelu_pair(dot(jnp.concatenate([part[...] for part in parts], axis=0), w_in[...]))
    hidden[...] = value.astype(BF16)
    slope[...] = grad


def grad_kernel(w_in, w_out, row_gate, row_slot, hid_a, slope_a, *refs):
    cots, boths = refs[:4], refs[4:8]
    hidden, grad_pre, gate_part, far = refs[8:]
    width = w_in.shape[0]
    early, late = cots[0].shape[0], boths[0].shape[0]
    count = early + late
    tok_b = jnp.concatenate([both[:, :width] for both in boths], axis=0)
    value_b, slope_b = gelu_pair(dot(tok_b, w_in[...]))
    value_b = value_b.astype(BF16)
    slopes = []
    for j in range(4):
        hidden[j * count : j * count + early, :] = hid_a[j * early : (j + 1) * early, :]
        hidden[j * count + early : (j + 1) * count, :] = value_b[j * late : (j + 1) * late, :]
        slopes += [slope_a[j * early : (j + 1) * early, :], slope_b[j * late : (j + 1) * late, :]]
    cot = jnp.concatenate(
        [part for j in range(4) for part in (cots[j][...], boths[j][:, width:])], axis=0
    )
    grad_out = dot(cot, w_out[...], 1, 1)
    pre = (grad_out * row_gate[...] * jnp.concatenate(slopes, axis=0)).astype(BF16)
    grad_pre[...] = pre
    per_row = jnp.sum(hidden[...].astype(F32) * grad_out, axis=1, keepdims=True)
    gate_part[...] = jnp.sum(jnp.where(row_slot[...] > 0, per_row, 0.0), axis=0, keepdims=True)
    step = 512
    for at in range(0, width, step):
        far[:, at : at + step] = dot(pre[3 * count :, :], w_in[at : at + step, :], 1, 1).astype(BF16)


def share_kernel(w_in, grad_pre, *pieces):
    count, width = pieces[0].shape
    step = 512
    for at in range(0, width, step):
        here = slice(at, at + step)
        share = dot(grad_pre[: 3 * count, :], w_in[here, :], 1, 1).astype(BF16)
        for j in range(3):
            pieces[j][:, here] = share[j * count : (j + 1) * count, :]


def weight_kernel(hidden, row_gate, grad_pre, *refs):
    tok_a, cot_a, both_b, (grad_in, grad_out) = refs[:4], refs[4:8], refs[8:12], refs[12:]
    gated = (hidden[...].astype(F32) * row_gate[...]).astype(BF16)
    width = grad_in.shape[0]
    step = 512
    for at in range(0, width, step):
        here = slice(at, at + step)
        late = [both[:, width + at : width + at + step] for both in both_b]
        cot = jnp.concatenate([part for j in range(4) for part in (cot_a[j][:, here], late[j])], axis=0)
        grad_out[:, here] = dot(gated, cot, 0, 0).astype(BF16)
        grad_in[here, :] = dot(stack(tok_a, both_b, at, step), grad_pre[...], 0, 0).astype(BF16)


def unpack_kernel(unpack, *refs):
    parts, out = refs[:4], refs[4]
    half = out.shape[1]
    matrix = unpack[...]
    side_of = iota(matrix.shape, 0) % 2
    total = jnp.zeros(out.shape, F32)
    for side in range(2):
        here = slice(side * half, (side + 1) * half)
        summed = parts[0][:, here].astype(F32)
        for other in parts[1:]:
            summed += other[:, here].astype(F32)
        total += dot(keep(side_of == side, matrix), summed.astype(BF16))
    out[...] = total.astype(BF16)


def token_kernel(picker, landed, out):
    tok_dev, width = out.shape
    half = width // 2
    for side in range(2):
        out[:, side * half : (side + 1) * half] = dot(
            picker[:, side * tok_dev : (side + 1) * tok_dev], landed[...], 0, 0
        ).astype(BF16)


def fullest(ids, tok_dev):
    experts, slots = ids.shape
    batch, side = 8, 16
    rows = batch * side
    digit = iota((rows, slots), 0) % side
    same = iota((rows, rows), 0) // side == iota((rows, rows), 1) // side
    column = iota((rows, rows), 0)
    target = iota((rows, rows), 1)
    fold = ones_where((column // side == target // 4) & (column % 4 == target % 4))
    best = jnp.zeros((8, rows), F32)
    for at in range(0, experts, batch):
        owner = jnp.concatenate(
            [jnp.broadcast_to(ids[e : e + 1, :] // tok_dev, (side, slots)) for e in range(at, at + batch)], axis=0
        )
        count = dot(ones_where(owner // side == digit), ones_where(owner % side == digit), 1, 1)
        extra = jnp.sum(jnp.where(same, jnp.maximum(count - 2.0, 0.0), 0.0), axis=0, keepdims=True)
        held = dot(jnp.broadcast_to(extra, (8, rows)).astype(BF16), fold)
        best = jnp.maximum(best, held)
    return jnp.max(best, axis=1, keepdims=True)


def shift(array, step):
    return lax.ppermute(array, "dp", [(d, (d + step) % 4) for d in range(4)])


def spread_rows(tok, cot):
    left_tok = shift(tok, 1)
    right_cot = shift(cot, -1)
    left_cot = shift(cot, 1)
    right_tok = shift(tok, -1)
    far_tok = shift(left_tok, 1)
    far_cot = shift(right_cot, -1)
    return (tok, left_tok, right_tok, far_tok), (cot, left_cot, right_cot, far_cot)


def exchange(array):
    return lax.all_to_all(array, "expert", split_axis=0, concat_axis=0, tiled=True)


def path(cap, place, everyone, my_ids, gate, w_in, w_out, picker, first, second):
    width, units = w_in.shape
    rows, half = first.shape
    slots = my_ids.shape[1]
    tok_dev = picker.shape[1] // 2
    level_rows = rows // 4
    landed_a = exchange(first)
    tok, cot = call(order_kernel, [shape_of(level_rows, width)] * 2, landed_a, flops=8 * level_rows * rows * half)
    tok, cot, second = lax.optimization_barrier((tok, cot, second))
    landed_b = exchange(second)
    toks_a, cots_a = spread_rows(tok, cot)
    everyone, tok = lax.optimization_barrier((everyone, tok))
    count = level_rows + cap
    row_slot, row_gate, pack, unpack, most = call(
        functools.partial(index_kernel, cap=cap, tok_dev=tok_dev),
        [
            shape_of(4 * count, slots),
            shape_of(4 * count, 1, dtype=F32),
            shape_of(cap, rows),
            shape_of(rows, count),
            shape_of(8, 128, dtype=jnp.int32),
        ],
        place, my_ids, gate, everyone, smem=1, flops=4 * cap * rows * slots,
    )
    both = call(pack_kernel, [shape_of(cap, 2 * width)], pack, landed_b, flops=8 * cap * rows * half)[0]
    both_b = (both, shift(both, 1), shift(both, -1), shift(both, 2))
    product = 2 * 4 * count * width * units
    hid_a, slope_a = call(
        hidden_kernel,
        [shape_of(4 * level_rows, units), shape_of(4 * level_rows, units, dtype=F32)],
        w_in, *toks_a, flops=product,
    )
    hidden, grad_pre, part, far = call(
        grad_kernel,
        [shape_of(4 * count, units)] * 2 + [shape_of(1, slots, dtype=F32), shape_of(count, width)],
        w_in, w_out, row_gate, row_slot, hid_a, slope_a, *cots_a, *both_b, flops=2 * product, mib=24,
    )
    own, left, right = call(share_kernel, [shape_of(count, width)] * 3, w_in, grad_pre, flops=product)
    far, left, right = shift(far, 2), shift(left, -1), shift(right, 1)
    back = call(
        unpack_kernel, [shape_of(rows, half)], unpack, own, left, right, far, flops=4 * count * rows * half
    )[0]
    merged = exchange(back)
    grad_gates = (part + shift(part, 2)) + (shift(part, 1) + shift(part, -1))
    grad_w_in, grad_w_out = call(
        weight_kernel,
        [shape_of(width, units), shape_of(units, width)],
        hidden, row_gate, grad_pre, *toks_a, *cots_a, *both_b, flops=2 * product,
    )
    grad_tokens = call(token_kernel, [shape_of(tok_dev, width)], picker, merged, flops=2 * tok_dev * rows * width)[0]
    return (grad_tokens, grad_w_in[None], grad_w_out[None], grad_gates), most


def body(tokens, cotangent, w_in, w_out, expert_tokens, gate_weights):
    tok_dev, width = tokens.shape
    experts, slots = expert_tokens.shape
    expert_idx = lax.axis_index("expert")
    dp_idx = lax.axis_index("dp")
    place = jnp.stack([expert_idx * 4 + dp_idx, dp_idx]).astype(jnp.int32)
    rows = experts * 8
    first, second, picker = call(
        send_kernel,
        [shape_of(rows, width // 2)] * 2 + [shape_of(rows, 2 * tok_dev)],
        place, expert_tokens, tokens, cotangent, smem=1, far=2,
        flops=4 * rows * tok_dev * width * 4,
        scratch=[pltpu.VMEM((4 * tok_dev, width // 2), BF16), pltpu.SemaphoreType.DMA((4,))], mib=56,
    )
    my_ids = lax.dynamic_slice_in_dim(expert_tokens, expert_idx, 1, 0)
    args = (place, expert_tokens, my_ids, gate_weights, w_in[0], w_out[0], picker, first, second)
    outs, most = path(SMALL, *args)
    state = lax.while_loop(
        lambda state: state[0] > SMALL,
        lambda state: (jnp.zeros((), jnp.int32), *path(2 * experts, *args)[0]),
        (most[0, 0], *outs),
    )
    return state[1:]


def solution(mesh):
    placed = (
        P(("expert", "dp"), None),
        P(("expert", "dp"), None),
        P("expert", None, "dp"),
        P("expert", "dp", None),
        P(),
        P("expert", None),
    )
    return jax.shard_map(
        body,
        mesh=mesh,
        in_specs=placed,
        out_specs=(
            P(("expert", "dp"), None),
            P("expert", None, "dp"),
            P("expert", "dp", None),
            P("expert", None),
        ),
        check_vma=False,
    )
```

```python
import functools

import jax
import jax.numpy as jnp
from jax import lax
from jax.experimental import pallas as pl
from jax.experimental.pallas import tpu as pltpu
from jax.sharding import PartitionSpec as P

GELU_SCALE = 0.7978845608028654
GELU_CUBIC = 0.044715
MOST = 4
BF16 = jnp.bfloat16
F32 = jnp.float32
VMEM = pl.BlockSpec(memory_space=pltpu.VMEM)
SMEM = pl.BlockSpec(memory_space=pltpu.SMEM)
HBM = pl.BlockSpec(memory_space=pltpu.HBM)
OFFSETS = (0, -1, 1, 2)
SMALL = (112, 48)
LONG = 10**11


def gelu_pair(pre_act):
    inner_arg = GELU_SCALE * (pre_act + GELU_CUBIC * pre_act * pre_act * pre_act)
    tanh_val = jnp.tanh(inner_arg)
    gelu_value = 0.5 * pre_act * (1.0 + tanh_val)
    gelu_slope = 0.5 * (1.0 + tanh_val) + 0.5 * pre_act * (
        1.0 - tanh_val * tanh_val
    ) * GELU_SCALE * (1.0 + 3.0 * GELU_CUBIC * pre_act * pre_act)
    return (gelu_value, gelu_slope)


def dot(a, b, da=1, db=0):
    return lax.dot_general(a, b, (((da,), (db,)), ((), ())), preferred_element_type=F32)


def iota(shape, dim):
    return lax.broadcasted_iota(jnp.int32, shape, dim)


def ones_where(mask):
    return jnp.where(mask, 1.0, 0.0).astype(BF16)


def keep(mask, array):
    return jnp.where(mask, array, jnp.zeros_like(array))


def call(kernel, outs, *args, flops=0, smem=0, far=0, scratch=(), mib=16):
    moved = sum(a.size * a.dtype.itemsize for a in (*args, *outs))
    return pl.pallas_call(
        kernel,
        out_shape=tuple(outs),
        in_specs=[SMEM] * smem + [VMEM] * (len(args) - smem - far) + [HBM] * far,
        out_specs=tuple(VMEM for _ in outs),
        scratch_shapes=list(scratch),
        compiler_params=pltpu.CompilerParams(vmem_limit_bytes=mib * 1024 * 1024),
        cost_estimate=pl.CostEstimate(flops=flops, bytes_accessed=moved, transcendentals=0),
    )(*args)


def shape_of(*dims, dtype=BF16):
    return jax.ShapeDtypeStruct(dims, dtype)


def running_count(mask):
    width = mask.shape[1]
    upper = ones_where(iota((width, width), 0) <= iota((width, width), 1))
    return dot(ones_where(mask), upper)


def send_kernel(place, ids, tokens, cotangent, first, two, picker, stacked, sems):
    experts, _ = ids.shape
    tok_dev, width = tokens.shape
    half = width // 2
    rows = experts * 8
    copies = []
    for q in range(4):
        source = (tokens, cotangent)[q // 2]
        copies.append(
            pltpu.make_async_copy(
                source.at[:, pl.ds(q % 2 * half, half)],
                stacked.at[pl.ds(q * tok_dev, tok_dev), :],
                sems.at[q],
            )
        )
        copies[-1].start()
    id_all = ids[...]
    owner = id_all // tok_dev
    local = id_all - owner * tok_dev
    mine = owner == place[0]
    rank = running_count(mine)
    lane = iota((experts, 128), 1)
    wanted = jnp.zeros((experts, 128), F32)
    for level in range(MOST):
        hit = mine & (rank == level + 1.0)
        found = jnp.sum(jnp.where(hit, local + 1, 0).astype(F32), axis=1, keepdims=True)
        wanted = jnp.where(lane == level, found, wanted)
    spread = ones_where(iota((rows, experts), 0) // 8 == iota((rows, experts), 1))
    by_row = dot(spread, wanted.astype(BF16))
    row = iota((rows, 128), 0) % 8
    lanes = iota((rows, 128), 1)

    def pick(level, part, parts):
        want = jnp.sum(jnp.where(level == lanes, by_row, 0.0), axis=1, keepdims=True)
        column = iota((rows, parts * tok_dev), 1)
        here = iota((rows, parts * tok_dev), 0) % 8
        return ones_where(
            (column // tok_dev == part(here)) & ((column % tok_dev + 1).astype(F32) == want)
        )

    one = pick(row // 4, lambda r: r % 4, 4)
    two[...] = pick(row // 4 + 2, lambda r: r % 4, 4)
    picker[...] = pick(row // 2, lambda r: r % 2, 2)
    for copy in copies:
        copy.wait()
    first[...] = dot(one, stacked[...]).astype(BF16)


def late_kernel(two, stacked, second):
    second[...] = dot(two[...], stacked[...]).astype(BF16)


def index_kernel(place, ids, gates, row_slot, row_gate, pack, unpack, *, caps, tok_dev):
    slots = ids.shape[1]
    rows = unpack.shape[0]
    experts = rows // 8
    my_dp = place[1]
    owner = ids[...] // tok_dev
    plane = owner % 4
    gate = gates[...]
    rank = jnp.zeros((1, slots), F32)
    for dp in range(4):
        from_owner = owner == iota((experts, slots), 0) * 4 + dp
        count = running_count(from_owner)
        rank += jnp.sum(jnp.where(from_owner, count, 0.0), axis=0, keepdims=True)
    block = iota((8, slots), 0)
    plane_of = jnp.zeros((8, slots), jnp.int32)
    for j, offset in enumerate(OFFSETS):
        plane_of = jnp.where(block == j, (my_dp + offset + 4) % 4, plane_of)
    on_plane = (plane_of == plane) & (block < 4)
    low = on_plane & (rank < 2.5)
    place_low = running_count(low)
    early = low & (place_low < caps[0] + 0.5)
    late = on_plane & ((rank > 2.5) | (place_low > caps[0] + 0.5))
    place_late = running_count(late)
    for j in range(4):
        at = j * sum(caps)
        for group, position, cap in ((early, place_low, caps[0]), (late, place_late, caps[1])):
            row = iota((cap, slots), 0).astype(F32) + 1.0
            hit = (position[j : j + 1, :] == row) & group[j : j + 1, :]
            here = slice(at, at + cap)
            row_slot[here, :] = ones_where(hit)
            row_gate[here, :] = jnp.sum(jnp.where(hit, gate, 0.0), axis=1, keepdims=True)
            at += cap
    row = iota((rows, slots), 0)
    on_row = owner == row // 8 * 4 + my_dp
    own = row_slot[: sum(caps), :]
    for part in range(2):
        arrived = ones_where(on_row & (rank == (row % 8 // 4 + 2 * part + 1).astype(F32)))
        pack[:, part * rows : (part + 1) * rows] = dot(own, arrived, 1, 1).astype(BF16)
    leaving = ones_where(on_row & (rank == (row % 8 // 2 + 1).astype(F32)))
    unpack[...] = dot(leaving, own, 1, 1).astype(BF16)


def count_kernel(everyone, picker, chosen, most, *, tok_dev):
    chosen[...] = picker[...].T
    most[...] = jnp.broadcast_to(fullest(everyone, tok_dev), most.shape).astype(jnp.int32)


def early_kernel(pack, landed, *outs):
    cap = outs[0].shape[0]
    rows, half = landed.shape
    matrix = pack[:cap, :rows]
    quarter = iota(matrix.shape, 1) % 4
    for q in range(4):
        outs[q // 2][:, q % 2 * half : (q % 2 + 1) * half] = dot(
            keep(quarter == q, matrix), landed[...]
        ).astype(BF16)


def pack_kernel(pack, landed_a, landed_b, *refs):
    both = refs[-1]
    cap = both.shape[0]
    rows, half = landed_a.shape
    early = pack.shape[0] - cap
    quarter = iota((cap, rows), 1) % 4
    for q in range(4):
        one = dot(keep(quarter == q, pack[early:, :rows]), landed_a[...])
        two = dot(keep(quarter == q, pack[early:, rows:]), landed_b[...])
        both[:, q * half : (q + 1) * half] = (one + two).astype(BF16)


def mixed(early, late):
    return jnp.concatenate([part for pair in zip(early, late) for part in pair], axis=0)


def grad_rows(w_in, w_out, tok, cot, gate, slot):
    value, slope = gelu_pair(dot(tok, w_in[...]))
    hidden = value.astype(BF16)
    grad_out = dot(cot, w_out[...], 1, 1)
    per_row = jnp.sum(hidden.astype(F32) * grad_out, axis=1, keepdims=True)
    part = jnp.sum(jnp.where(slot > 0, per_row, 0.0), axis=0, keepdims=True)
    return hidden, (grad_out * gate * slope).astype(BF16), part


def cut(ref, first, size, count):
    return jnp.concatenate([ref[j * count + first : j * count + first + size, :] for j in range(4)], axis=0)


def main_kernel(w_in, w_out, row_gate, row_slot, *refs):
    toks, cots, (hidden, grad_pre, part) = refs[:4], refs[4:8], refs[8:]
    early = toks[0].shape[0]
    count = row_gate.shape[0] // 4
    tok = jnp.concatenate([part_of[...] for part_of in toks], axis=0)
    cot = jnp.concatenate([part_of[...] for part_of in cots], axis=0)
    gate = cut(row_gate, 0, early, count)
    hidden[...], grad_pre[...], part[...] = grad_rows(
        w_in, w_out, tok, cot, gate, cut(row_slot, 0, early, count)
    )


def rest_kernel(w_in, w_out, row_gate, row_slot, hid_a, pre_a, part_a, *refs):
    boths, (hidden, grad_pre, part, far0, far1) = refs[:4], refs[4:]
    width = w_in.shape[0]
    late = boths[0].shape[0]
    count = row_gate.shape[0] // 4
    early = count - late
    tok = jnp.concatenate([both[:, :width] for both in boths], axis=0)
    cot = jnp.concatenate([both[:, width:] for both in boths], axis=0)
    hid_b, pre_b, part_b = grad_rows(
        w_in, w_out, tok, cot, cut(row_gate, early, late, count), cut(row_slot, early, late, count)
    )
    part[...] = part_a[...] + part_b
    for j in range(4):
        for out, one, two in ((hidden, hid_a, hid_b), (grad_pre, pre_a, pre_b)):
            out[j * count : j * count + early, :] = one[j * early : (j + 1) * early, :]
            out[j * count + early : (j + 1) * count, :] = two[j * late : (j + 1) * late, :]
    half = width // 2
    far0[...] = dot(grad_pre[3 * count :, :], w_in[:half, :], 1, 1).astype(BF16)
    far1[...] = dot(grad_pre[3 * count :, :], w_in[half:, :], 1, 1).astype(BF16)


def share_kernel(w_in, grad_pre, *pieces):
    count, half = pieces[0].shape
    for side in range(2):
        share = dot(grad_pre[: 3 * count, :], w_in[side * half : (side + 1) * half, :], 1, 1).astype(BF16)
        for j in range(3):
            pieces[2 * j + side][...] = share[j * count : (j + 1) * count, :]


def weight_kernel(hidden, row_gate, grad_pre, *refs):
    tok_a, cot_a, both_b, (grad_in, grad_out) = refs[:4], refs[4:8], refs[8:12], refs[12:]
    gated = (hidden[...].astype(F32) * row_gate[...]).astype(BF16)
    width = grad_in.shape[0]
    step = 512
    for at in range(0, width, step):
        here = slice(at, at + step)
        late = [both[:, width + at : width + at + step] for both in both_b]
        cot = mixed([near[:, here] for near in cot_a], late)
        grad_out[:, here] = dot(gated, cot, 0, 0).astype(BF16)
        tok = mixed([near[:, here] for near in tok_a], [both[:, here] for both in both_b])
        grad_in[here, :] = dot(tok, grad_pre[...], 0, 0).astype(BF16)


def unpack_kernel(unpack, *refs):
    parts, out = refs[:6], refs[6]
    half = out.shape[1]
    matrix = unpack[...]
    side_of = iota(matrix.shape, 0) % 2
    total = jnp.zeros(out.shape, F32)
    for side in range(2):
        summed = sum(part[...].astype(F32) for part in parts[side::2])
        total += dot(keep(side_of == side, matrix), summed.astype(BF16))
    out[...] = total.astype(BF16)


def token_kernel(chosen, landed, out):
    tok_dev, width = out.shape
    half = width // 2
    for side in range(2):
        out[:, side * half : (side + 1) * half] = dot(
            chosen[side * tok_dev : (side + 1) * tok_dev, :], landed[...]
        ).astype(BF16)


def fullest(ids, tok_dev):
    experts, slots = ids.shape
    batch, side = 8, 16
    rows = batch * side
    digit = iota((rows, slots), 0) % side
    same = iota((rows, rows), 0) // side == iota((rows, rows), 1) // side
    column = iota((rows, rows), 0)
    target = iota((rows, rows), 1)
    fold = ones_where((column // side == target // 4) & (column % 4 == target % 4))
    best = jnp.zeros((8, rows), F32)
    for at in range(0, experts, batch):
        owner = jnp.concatenate(
            [jnp.broadcast_to(ids[e : e + 1, :] // tok_dev, (side, slots)) for e in range(at, at + batch)], axis=0
        )
        count = dot(ones_where(owner // side == digit), ones_where(owner % side == digit), 1, 1)
        low = jnp.sum(jnp.where(same, jnp.minimum(count, 2.0), 0.0), axis=0, keepdims=True)
        high = jnp.sum(jnp.where(same, jnp.maximum(count - 2.0, 0.0), 0.0), axis=0, keepdims=True)
        low = dot(jnp.broadcast_to(low, (8, rows)).astype(BF16), fold)
        high = dot(jnp.broadcast_to(high, (8, rows)).astype(BF16), fold)
        best = jnp.maximum(best, high + jnp.maximum(low - SMALL[0], 0.0))
    return jnp.max(best, axis=1, keepdims=True)


def shift(array, step):
    return lax.ppermute(array, "dp", [(d, (d + step) % 4) for d in range(4)])


def add(one, two):
    return (one.astype(F32) + two.astype(F32)).astype(BF16)


def exchange(array):
    return lax.all_to_all(array, "expert", split_axis=0, concat_axis=0, tiled=True)


def path(caps, place, everyone, my_ids, gate, w_in, w_out, picker, first, second):
    width, units = w_in.shape
    rows, half = first.shape
    slots = my_ids.shape[1]
    tok_dev = picker.shape[1] // 2
    early, late = caps
    count = early + late
    landed_a = exchange(first)
    row_slot, row_gate, pack, unpack = call(
        functools.partial(index_kernel, caps=caps, tok_dev=tok_dev),
        [
            shape_of(4 * count, slots),
            shape_of(4 * count, 1, dtype=F32),
            shape_of(count, 2 * rows),
            shape_of(rows, count),
        ],
        place, my_ids, gate, smem=1, flops=4 * count * rows * slots,
    )
    tok, cot = call(early_kernel, [shape_of(early, width)] * 2, pack, landed_a, flops=LONG)
    landed_b = exchange(second)
    left_tok, right_cot = shift(tok, 1), shift(cot, -1)
    left_cot, right_tok = shift(cot, 1), shift(tok, -1)
    chosen, most = call(
        functools.partial(count_kernel, tok_dev=tok_dev),
        [shape_of(2 * tok_dev, rows), shape_of(8, 128, dtype=jnp.int32)], everyone, picker, flops=LONG,
    )
    left_tok, chosen = lax.optimization_barrier((left_tok, chosen))
    right_cot, most = lax.optimization_barrier((right_cot, most))
    toks_a = (tok, left_tok, right_tok, shift(left_tok, 1))
    cots_a = (cot, left_cot, right_cot, shift(right_cot, -1))
    both = call(
        pack_kernel, [shape_of(late, 2 * width)], pack, landed_a, landed_b, left_tok, right_cot, far=2, flops=LONG
    )[0]
    both_b = (both, shift(both, 1), shift(both, -1), shift(both, 2))
    product = 2 * 4 * count * width * units
    piece = shape_of(count, half)
    gate_sum = shape_of(1, slots, dtype=F32)
    main = call(
        main_kernel, [shape_of(4 * early, units)] * 2 + [gate_sum],
        w_in, w_out, row_gate, row_slot, *toks_a, *cots_a, flops=LONG, mib=24,
    )
    hidden, grad_pre, part, far0, far1 = call(
        rest_kernel, [shape_of(4 * count, units)] * 2 + [gate_sum] + [piece] * 2,
        w_in, w_out, row_gate, row_slot, *main, *both_b, flops=product,
    )
    far0, far1 = shift(far0, 1), shift(far1, -1)
    own0, own1, left0, left1, right0, right1 = call(share_kernel, [piece] * 6, w_in, grad_pre, flops=product)
    right1, left0 = shift(right1, 1), shift(left0, -1)
    right0, left1 = shift(add(right0, far0), 1), shift(add(left1, far1), -1)
    back = call(
        unpack_kernel, [shape_of(rows, half)], unpack, own0, own1, left0, left1, right0, right1,
        flops=4 * count * rows * half,
    )[0]
    merged = exchange(back)
    grad_gates = (part + shift(part, 2)) + (shift(part, 1) + shift(part, -1))
    grad_w_in, grad_w_out = call(
        weight_kernel,
        [shape_of(width, units), shape_of(units, width)],
        hidden, row_gate, grad_pre, *toks_a, *cots_a, *both_b, flops=2 * product,
    )
    grad_tokens = call(token_kernel, [shape_of(tok_dev, width)], chosen, merged, flops=2 * tok_dev * rows * width)[0]
    return (grad_tokens, grad_w_in[None], grad_w_out[None], grad_gates), most


def body(tokens, cotangent, w_in, w_out, expert_tokens, gate_weights):
    tok_dev, width = tokens.shape
    experts, slots = expert_tokens.shape
    expert_idx = lax.axis_index("expert")
    dp_idx = lax.axis_index("dp")
    place = jnp.stack([expert_idx * 4 + dp_idx, dp_idx]).astype(jnp.int32)
    rows = experts * 8
    first, two, picker, stacked = call(
        send_kernel,
        [
            shape_of(rows, width // 2),
            shape_of(rows, 4 * tok_dev),
            shape_of(rows, 2 * tok_dev),
            shape_of(4 * tok_dev, width // 2),
        ],
        place, expert_tokens, tokens, cotangent, smem=1, far=2,
        flops=2 * rows * tok_dev * width * 4,
        scratch=[pltpu.SemaphoreType.DMA((4,))], mib=56,
    )
    second = call(late_kernel, [shape_of(rows, width // 2)], two, stacked, flops=2 * rows * rows * width)[0]
    my_ids = lax.dynamic_slice_in_dim(expert_tokens, expert_idx, 1, 0)
    args = (place, expert_tokens, my_ids, gate_weights, w_in[0], w_out[0], picker, first, second)
    outs, most = path(SMALL, *args)
    state = lax.while_loop(
        lambda state: state[0] > SMALL[1],
        lambda state: (jnp.zeros((), jnp.int32), *path((2 * experts, 2 * experts), *args)[0]),
        (most[0, 0], *outs),
    )
    return state[1:]


def solution(mesh):
    placed = (
        P(("expert", "dp"), None),
        P(("expert", "dp"), None),
        P("expert", None, "dp"),
        P("expert", "dp", None),
        P(),
        P("expert", None),
    )
    return jax.shard_map(
        body,
        mesh=mesh,
        in_specs=placed,
        out_specs=(
            P(("expert", "dp"), None),
            P("expert", None, "dp"),
            P("expert", "dp", None),
            P("expert", None),
        ),
        check_vma=False,
    )
```

```python
import functools

import jax
import jax.numpy as jnp
from jax import lax
from jax.experimental import pallas as pl
from jax.experimental.pallas import tpu as pltpu
from jax.sharding import PartitionSpec as P

GELU_SCALE = 0.7978845608028654
GELU_CUBIC = 0.044715
MOST = 4
BF16 = jnp.bfloat16
F32 = jnp.float32
VMEM = pl.BlockSpec(memory_space=pltpu.VMEM)
SMEM = pl.BlockSpec(memory_space=pltpu.SMEM)
HBM = pl.BlockSpec(memory_space=pltpu.HBM)
OFFSETS = (0, -1, 1, 2)
SMALL = (112, 48)
LONG = 10**11


def gelu_pair(pre_act):
    inner_arg = GELU_SCALE * (pre_act + GELU_CUBIC * pre_act * pre_act * pre_act)
    tanh_val = jnp.tanh(inner_arg)
    gelu_value = 0.5 * pre_act * (1.0 + tanh_val)
    gelu_slope = 0.5 * (1.0 + tanh_val) + 0.5 * pre_act * (
        1.0 - tanh_val * tanh_val
    ) * GELU_SCALE * (1.0 + 3.0 * GELU_CUBIC * pre_act * pre_act)
    return (gelu_value, gelu_slope)


def dot(a, b, da=1, db=0):
    return lax.dot_general(a, b, (((da,), (db,)), ((), ())), preferred_element_type=F32)


def iota(shape, dim):
    return lax.broadcasted_iota(jnp.int32, shape, dim)


def ones_where(mask):
    return jnp.where(mask, 1.0, 0.0).astype(BF16)


def keep(mask, array):
    return jnp.where(mask, array, jnp.zeros_like(array))


def call(kernel, outs, *args, flops=0, smem=0, far=0, scratch=(), mib=16):
    moved = sum(a.size * a.dtype.itemsize for a in (*args, *outs))
    return pl.pallas_call(
        kernel,
        out_shape=tuple(outs),
        in_specs=[SMEM] * smem + [VMEM] * (len(args) - smem - far) + [HBM] * far,
        out_specs=tuple(VMEM for _ in outs),
        scratch_shapes=list(scratch),
        compiler_params=pltpu.CompilerParams(vmem_limit_bytes=mib * 1024 * 1024),
        cost_estimate=pl.CostEstimate(flops=flops, bytes_accessed=moved, transcendentals=0),
    )(*args)


def shape_of(*dims, dtype=BF16):
    return jax.ShapeDtypeStruct(dims, dtype)


def running_count(mask):
    width = mask.shape[1]
    upper = ones_where(iota((width, width), 0) <= iota((width, width), 1))
    return dot(ones_where(mask), upper)


def send_kernel(place, ids, tokens, cotangent, first, two, picker, stacked, sems):
    experts, _ = ids.shape
    tok_dev, width = tokens.shape
    half = width // 2
    rows = experts * 8
    copies = []
    for q in range(4):
        source = (tokens, cotangent)[q // 2]
        copies.append(
            pltpu.make_async_copy(
                source.at[:, pl.ds(q % 2 * half, half)],
                stacked.at[pl.ds(q * tok_dev, tok_dev), :],
                sems.at[q],
            )
        )
        copies[-1].start()
    id_all = ids[...]
    owner = id_all // tok_dev
    local = id_all - owner * tok_dev
    mine = owner == place[0]
    rank = running_count(mine)
    lane = iota((experts, 128), 1)
    wanted = jnp.zeros((experts, 128), F32)
    for level in range(MOST):
        hit = mine & (rank == level + 1.0)
        found = jnp.sum(jnp.where(hit, local + 1, 0).astype(F32), axis=1, keepdims=True)
        wanted = jnp.where(lane == level, found, wanted)
    spread = ones_where(iota((rows, experts), 0) // 8 == iota((rows, experts), 1))
    by_row = dot(spread, wanted.astype(BF16))
    row = iota((rows, 128), 0) % 8
    lanes = iota((rows, 128), 1)

    def pick(level, part, parts):
        want = jnp.sum(jnp.where(level == lanes, by_row, 0.0), axis=1, keepdims=True)
        column = iota((rows, parts * tok_dev), 1)
        here = iota((rows, parts * tok_dev), 0) % 8
        return ones_where(
            (column // tok_dev == part(here)) & ((column % tok_dev + 1).astype(F32) == want)
        )

    one = pick(row // 4, lambda r: r % 4, 4)
    two[...] = pick(row // 4 + 2, lambda r: r % 4, 4)
    picker[...] = pick(row // 2, lambda r: r % 2, 2)
    for copy in copies:
        copy.wait()
    first[...] = dot(one, stacked[...]).astype(BF16)


def late_kernel(two, stacked, second):
    second[...] = dot(two[...], stacked[...]).astype(BF16)


def index_kernel(place, ids, gates, row_slot, row_gate, pack, unpack, *, caps, tok_dev):
    slots = ids.shape[1]
    rows = unpack.shape[0]
    experts = rows // 8
    my_dp = place[1]
    owner = ids[...] // tok_dev
    plane = owner % 4
    gate = gates[...]
    rank = jnp.zeros((1, slots), F32)
    for dp in range(4):
        from_owner = owner == iota((experts, slots), 0) * 4 + dp
        count = running_count(from_owner)
        rank += jnp.sum(jnp.where(from_owner, count, 0.0), axis=0, keepdims=True)
    block = iota((8, slots), 0)
    plane_of = jnp.zeros((8, slots), jnp.int32)
    for j, offset in enumerate(OFFSETS):
        plane_of = jnp.where(block == j, (my_dp + offset + 4) % 4, plane_of)
    on_plane = (plane_of == plane) & (block < 4)
    low = on_plane & (rank < 2.5)
    place_low = running_count(low)
    early = low & (place_low < caps[0] + 0.5)
    late = on_plane & ((rank > 2.5) | (place_low > caps[0] + 0.5))
    place_late = running_count(late)
    for j in range(4):
        at = j * sum(caps)
        for group, position, cap in ((early, place_low, caps[0]), (late, place_late, caps[1])):
            row = iota((cap, slots), 0).astype(F32) + 1.0
            hit = (position[j : j + 1, :] == row) & group[j : j + 1, :]
            here = slice(at, at + cap)
            row_slot[here, :] = ones_where(hit)
            row_gate[here, :] = jnp.sum(jnp.where(hit, gate, 0.0), axis=1, keepdims=True)
            at += cap
    row = iota((rows, slots), 0)
    on_row = owner == row // 8 * 4 + my_dp
    own = row_slot[: sum(caps), :]
    for part in range(2):
        arrived = ones_where(on_row & (rank == (row % 8 // 4 + 2 * part + 1).astype(F32)))
        pack[:, part * rows : (part + 1) * rows] = dot(own, arrived, 1, 1).astype(BF16)
    leaving = ones_where(on_row & (rank == (row % 8 // 2 + 1).astype(F32)))
    unpack[...] = dot(leaving, own, 1, 1).astype(BF16)


def count_kernel(everyone, picker, chosen, most, *, tok_dev):
    chosen[...] = picker[...].T
    most[...] = jnp.broadcast_to(fullest(everyone, tok_dev), most.shape).astype(jnp.int32)


def early_kernel(pack, landed, *outs):
    cap = outs[0].shape[0]
    rows, half = landed.shape
    matrix = pack[:cap, :rows]
    quarter = iota(matrix.shape, 1) % 4
    for q in range(4):
        outs[q // 2][:, q % 2 * half : (q % 2 + 1) * half] = dot(
            keep(quarter == q, matrix), landed[...]
        ).astype(BF16)


def pack_kernel(pack, landed_a, landed_b, *refs):
    outs = refs[-2:]
    cap = outs[0].shape[0]
    rows, half = landed_a.shape
    early = pack.shape[0] - cap
    quarter = iota((cap, rows), 1) % 4
    for q in range(4):
        one = dot(keep(quarter == q, pack[early:, :rows]), landed_a[...])
        two = dot(keep(quarter == q, pack[early:, rows:]), landed_b[...])
        outs[q // 2][:, q % 2 * half : (q % 2 + 1) * half] = (one + two).astype(BF16)


def mixed(early, late):
    return jnp.concatenate([part for pair in zip(early, late) for part in pair], axis=0)


def grad_rows(w_in, w_out, tok, cot, gate, slot):
    value, slope = gelu_pair(dot(tok, w_in[...]))
    hidden = value.astype(BF16)
    grad_out = dot(cot, w_out[...], 1, 1)
    per_row = jnp.sum(hidden.astype(F32) * grad_out, axis=1, keepdims=True)
    part = jnp.sum(jnp.where(slot > 0, per_row, 0.0), axis=0, keepdims=True)
    return hidden, (grad_out * gate * slope).astype(BF16), part


def cut(ref, first, size, count):
    return jnp.concatenate([ref[j * count + first : j * count + first + size, :] for j in range(4)], axis=0)


def main_kernel(w_in, w_out, row_gate, row_slot, *refs):
    toks, cots, (hidden, grad_pre, part) = refs[:4], refs[4:8], refs[8:]
    early = toks[0].shape[0]
    count = row_gate.shape[0] // 4
    tok = jnp.concatenate([part_of[...] for part_of in toks], axis=0)
    cot = jnp.concatenate([part_of[...] for part_of in cots], axis=0)
    gate = cut(row_gate, 0, early, count)
    hidden[...], grad_pre[...], part[...] = grad_rows(
        w_in, w_out, tok, cot, gate, cut(row_slot, 0, early, count)
    )


def rest_kernel(w_in, w_out, row_gate, row_slot, hid_a, pre_a, part_a, *refs):
    toks, cots, (hidden, grad_pre, part, far0, far1) = refs[:4], refs[4:8], refs[8:]
    width = w_in.shape[0]
    late = toks[0].shape[0]
    count = row_gate.shape[0] // 4
    early = count - late
    tok = jnp.concatenate([part_of[...] for part_of in toks], axis=0)
    cot = jnp.concatenate([part_of[...] for part_of in cots], axis=0)
    hid_b, pre_b, part_b = grad_rows(
        w_in, w_out, tok, cot, cut(row_gate, early, late, count), cut(row_slot, early, late, count)
    )
    part[...] = part_a[...] + part_b
    for j in range(4):
        for out, one, two in ((hidden, hid_a, hid_b), (grad_pre, pre_a, pre_b)):
            out[j * count : j * count + early, :] = one[j * early : (j + 1) * early, :]
            out[j * count + early : (j + 1) * count, :] = two[j * late : (j + 1) * late, :]
    half = width // 2
    far0[...] = dot(grad_pre[3 * count :, :], w_in[:half, :], 1, 1).astype(BF16)
    far1[...] = dot(grad_pre[3 * count :, :], w_in[half:, :], 1, 1).astype(BF16)


def share_kernel(w_in, grad_pre, *pieces):
    count, half = pieces[0].shape
    for side in range(2):
        share = dot(grad_pre[: 3 * count, :], w_in[side * half : (side + 1) * half, :], 1, 1).astype(BF16)
        for j in range(3):
            pieces[2 * j + side][...] = share[j * count : (j + 1) * count, :]


def weight_kernel(hidden, row_gate, grad_pre, *refs):
    tok_a, cot_a, tok_b, cot_b = refs[:4], refs[4:8], refs[8:12], refs[12:16]
    grad_in, grad_out = refs[16:]
    gated = (hidden[...].astype(F32) * row_gate[...]).astype(BF16)
    width = grad_in.shape[0]
    step = 512
    for at in range(0, width, step):
        here = slice(at, at + step)
        cot = mixed([near[:, here] for near in cot_a], [near[:, here] for near in cot_b])
        grad_out[:, here] = dot(gated, cot, 0, 0).astype(BF16)
        tok = mixed([near[:, here] for near in tok_a], [near[:, here] for near in tok_b])
        grad_in[here, :] = dot(tok, grad_pre[...], 0, 0).astype(BF16)


def unpack_kernel(unpack, *refs):
    parts, out = refs[:6], refs[6]
    half = out.shape[1]
    matrix = unpack[...]
    side_of = iota(matrix.shape, 0) % 2
    total = jnp.zeros(out.shape, F32)
    for side in range(2):
        summed = sum(part[...].astype(F32) for part in parts[side::2])
        total += dot(keep(side_of == side, matrix), summed.astype(BF16))
    out[...] = total.astype(BF16)


def token_kernel(chosen, landed, out):
    tok_dev, width = out.shape
    half = width // 2
    for side in range(2):
        out[:, side * half : (side + 1) * half] = dot(
            chosen[side * tok_dev : (side + 1) * tok_dev, :], landed[...]
        ).astype(BF16)


def fullest(ids, tok_dev):
    experts, slots = ids.shape
    batch, side = 8, 16
    rows = batch * side
    digit = iota((rows, slots), 0) % side
    same = iota((rows, rows), 0) // side == iota((rows, rows), 1) // side
    column = iota((rows, rows), 0)
    target = iota((rows, rows), 1)
    fold = ones_where((column // side == target // 4) & (column % 4 == target % 4))
    best = jnp.zeros((8, rows), F32)
    for at in range(0, experts, batch):
        owner = jnp.concatenate(
            [jnp.broadcast_to(ids[e : e + 1, :] // tok_dev, (side, slots)) for e in range(at, at + batch)], axis=0
        )
        count = dot(ones_where(owner // side == digit), ones_where(owner % side == digit), 1, 1)
        low = jnp.sum(jnp.where(same, jnp.minimum(count, 2.0), 0.0), axis=0, keepdims=True)
        high = jnp.sum(jnp.where(same, jnp.maximum(count - 2.0, 0.0), 0.0), axis=0, keepdims=True)
        low = dot(jnp.broadcast_to(low, (8, rows)).astype(BF16), fold)
        high = dot(jnp.broadcast_to(high, (8, rows)).astype(BF16), fold)
        best = jnp.maximum(best, high + jnp.maximum(low - SMALL[0], 0.0))
    return jnp.max(best, axis=1, keepdims=True)


def shift(array, step):
    return lax.ppermute(array, "dp", [(d, (d + step) % 4) for d in range(4)])


def add(one, two):
    return (one.astype(F32) + two.astype(F32)).astype(BF16)


def exchange(array):
    return lax.all_to_all(array, "expert", split_axis=0, concat_axis=0, tiled=True)


def path(caps, place, everyone, my_ids, gate, w_in, w_out, picker, first, second):
    width, units = w_in.shape
    rows, half = first.shape
    slots = my_ids.shape[1]
    tok_dev = picker.shape[1] // 2
    early, late = caps
    count = early + late
    landed_a = exchange(first)
    row_slot, row_gate, pack, unpack = call(
        functools.partial(index_kernel, caps=caps, tok_dev=tok_dev),
        [
            shape_of(4 * count, slots),
            shape_of(4 * count, 1, dtype=F32),
            shape_of(count, 2 * rows),
            shape_of(rows, count),
        ],
        place, my_ids, gate, smem=1, flops=4 * count * rows * slots,
    )
    tok, cot = call(early_kernel, [shape_of(early, width)] * 2, pack, landed_a, flops=LONG)
    landed_b = exchange(second)
    left_tok, right_cot = shift(tok, 1), shift(cot, -1)
    left_cot, right_tok = shift(cot, 1), shift(tok, -1)
    chosen, most = call(
        functools.partial(count_kernel, tok_dev=tok_dev),
        [shape_of(2 * tok_dev, rows), shape_of(8, 128, dtype=jnp.int32)], everyone, picker, flops=LONG // 10,
    )
    left_tok, chosen = lax.optimization_barrier((left_tok, chosen))
    right_cot, most = lax.optimization_barrier((right_cot, most))
    toks_a = (tok, left_tok, right_tok, shift(left_tok, 1))
    cots_a = (cot, left_cot, right_cot, shift(right_cot, -1))
    tok, cot = call(
        pack_kernel, [shape_of(late, width)] * 2, pack, landed_a, landed_b, left_tok, right_cot, far=2, flops=LONG
    )
    left_tok, right_cot = shift(tok, 1), shift(cot, -1)
    left_cot, right_tok = shift(cot, 1), shift(tok, -1)
    toks_b = (tok, left_tok, right_tok, shift(left_tok, 1))
    cots_b = (cot, left_cot, right_cot, shift(right_cot, -1))
    product = 2 * 4 * count * width * units
    piece = shape_of(count, half)
    gate_sum = shape_of(1, slots, dtype=F32)
    main = call(
        main_kernel, [shape_of(4 * early, units)] * 2 + [gate_sum],
        w_in, w_out, row_gate, row_slot, *toks_a, *cots_a, flops=LONG, mib=24,
    )
    hidden, grad_pre, part, far0, far1 = call(
        rest_kernel, [shape_of(4 * count, units)] * 2 + [gate_sum] + [piece] * 2,
        w_in, w_out, row_gate, row_slot, *main, *toks_b, *cots_b, flops=product,
    )
    far0, far1 = shift(far0, 1), shift(far1, -1)
    own0, own1, left0, left1, right0, right1 = call(share_kernel, [piece] * 6, w_in, grad_pre, flops=product)
    right1, left0 = shift(right1, 1), shift(left0, -1)
    right0, left1 = shift(add(right0, far0), 1), shift(add(left1, far1), -1)
    back = call(
        unpack_kernel, [shape_of(rows, half)], unpack, own0, own1, left0, left1, right0, right1,
        flops=4 * count * rows * half,
    )[0]
    merged = exchange(back)
    grad_gates = (part + shift(part, 2)) + (shift(part, 1) + shift(part, -1))
    grad_w_in, grad_w_out = call(
        weight_kernel,
        [shape_of(width, units), shape_of(units, width)],
        hidden, row_gate, grad_pre, *toks_a, *cots_a, *toks_b, *cots_b, flops=2 * product,
    )
    grad_tokens = call(token_kernel, [shape_of(tok_dev, width)], chosen, merged, flops=2 * tok_dev * rows * width)[0]
    return (grad_tokens, grad_w_in[None], grad_w_out[None], grad_gates), most


def body(tokens, cotangent, w_in, w_out, expert_tokens, gate_weights):
    tok_dev, width = tokens.shape
    experts, slots = expert_tokens.shape
    expert_idx = lax.axis_index("expert")
    dp_idx = lax.axis_index("dp")
    place = jnp.stack([expert_idx * 4 + dp_idx, dp_idx]).astype(jnp.int32)
    rows = experts * 8
    first, two, picker, stacked = call(
        send_kernel,
        [
            shape_of(rows, width // 2),
            shape_of(rows, 4 * tok_dev),
            shape_of(rows, 2 * tok_dev),
            shape_of(4 * tok_dev, width // 2),
        ],
        place, expert_tokens, tokens, cotangent, smem=1, far=2,
        flops=2 * rows * tok_dev * width * 4,
        scratch=[pltpu.SemaphoreType.DMA((4,))], mib=56,
    )
    second = call(late_kernel, [shape_of(rows, width // 2)], two, stacked, flops=2 * rows * rows * width)[0]
    my_ids = lax.dynamic_slice_in_dim(expert_tokens, expert_idx, 1, 0)
    args = (place, expert_tokens, my_ids, gate_weights, w_in[0], w_out[0], picker, first, second)
    outs, most = path(SMALL, *args)
    state = lax.while_loop(
        lambda state: state[0] > SMALL[1],
        lambda state: (jnp.zeros((), jnp.int32), *path((2 * experts, 2 * experts), *args)[0]),
        (most[0, 0], *outs),
    )
    return state[1:]


def solution(mesh):
    placed = (
        P(("expert", "dp"), None),
        P(("expert", "dp"), None),
        P("expert", None, "dp"),
        P("expert", "dp", None),
        P(),
        P("expert", None),
    )
    return jax.shard_map(
        body,
        mesh=mesh,
        in_specs=placed,
        out_specs=(
            P(("expert", "dp"), None),
            P("expert", None, "dp"),
            P("expert", "dp", None),
            P("expert", None),
        ),
        check_vma=False,
    )
```

```python
import functools

import jax
import jax.numpy as jnp
from jax import lax
from jax.experimental import pallas as pl
from jax.experimental.pallas import tpu as pltpu
from jax.sharding import PartitionSpec as P

GELU_SCALE = 0.7978845608028654
GELU_CUBIC = 0.044715
MOST = 4
BF16 = jnp.bfloat16
F32 = jnp.float32
VMEM = pl.BlockSpec(memory_space=pltpu.VMEM)
SMEM = pl.BlockSpec(memory_space=pltpu.SMEM)
HBM = pl.BlockSpec(memory_space=pltpu.HBM)
OFFSETS = (0, -1, 1, 2)
SMALL = (112, 48)
LONG = 3 * 10**10


def gelu_pair(pre_act):
    inner_arg = GELU_SCALE * (pre_act + GELU_CUBIC * pre_act * pre_act * pre_act)
    tanh_val = jnp.tanh(inner_arg)
    gelu_value = 0.5 * pre_act * (1.0 + tanh_val)
    gelu_slope = 0.5 * (1.0 + tanh_val) + 0.5 * pre_act * (
        1.0 - tanh_val * tanh_val
    ) * GELU_SCALE * (1.0 + 3.0 * GELU_CUBIC * pre_act * pre_act)
    return (gelu_value, gelu_slope)


def dot(a, b, da=1, db=0):
    return lax.dot_general(a, b, (((da,), (db,)), ((), ())), preferred_element_type=F32)


def iota(shape, dim):
    return lax.broadcasted_iota(jnp.int32, shape, dim)


def ones_where(mask):
    return jnp.where(mask, 1.0, 0.0).astype(BF16)


def keep(mask, array):
    return jnp.where(mask, array, jnp.zeros_like(array))


def call(kernel, outs, *args, flops=0, smem=0, far=0, scratch=(), mib=16):
    moved = sum(a.size * a.dtype.itemsize for a in (*args, *outs))
    return pl.pallas_call(
        kernel,
        out_shape=tuple(outs),
        in_specs=[SMEM] * smem + [VMEM] * (len(args) - smem - far) + [HBM] * far,
        out_specs=tuple(VMEM for _ in outs),
        scratch_shapes=list(scratch),
        compiler_params=pltpu.CompilerParams(vmem_limit_bytes=mib * 1024 * 1024),
        cost_estimate=pl.CostEstimate(flops=flops, bytes_accessed=moved, transcendentals=0),
    )(*args)


def shape_of(*dims, dtype=BF16):
    return jax.ShapeDtypeStruct(dims, dtype)


def running_count(mask):
    width = mask.shape[1]
    upper = ones_where(iota((width, width), 0) <= iota((width, width), 1))
    return dot(ones_where(mask), upper)


def send_kernel(place, ids, tokens, cotangent, first, two, picker, stacked, sems):
    experts, _ = ids.shape
    tok_dev, width = tokens.shape
    half = width // 2
    rows = experts * 8
    copies = []
    for q in range(4):
        source = (tokens, cotangent)[q // 2]
        copies.append(
            pltpu.make_async_copy(
                source.at[:, pl.ds(q % 2 * half, half)],
                stacked.at[pl.ds(q * tok_dev, tok_dev), :],
                sems.at[q],
            )
        )
        copies[-1].start()
    id_all = ids[...]
    owner = id_all // tok_dev
    local = id_all - owner * tok_dev
    mine = owner == place[0]
    rank = running_count(mine)
    lane = iota((experts, 128), 1)
    wanted = jnp.zeros((experts, 128), F32)
    for level in range(MOST):
        hit = mine & (rank == level + 1.0)
        found = jnp.sum(jnp.where(hit, local + 1, 0).astype(F32), axis=1, keepdims=True)
        wanted = jnp.where(lane == level, found, wanted)
    spread = ones_where(iota((rows, experts), 0) // 8 == iota((rows, experts), 1))
    by_row = dot(spread, wanted.astype(BF16))
    row = iota((rows, 128), 0) % 8
    lanes = iota((rows, 128), 1)

    def pick(level, part, parts):
        want = jnp.sum(jnp.where(level == lanes, by_row, 0.0), axis=1, keepdims=True)
        column = iota((rows, parts * tok_dev), 1)
        here = iota((rows, parts * tok_dev), 0) % 8
        return ones_where(
            (column // tok_dev == part(here)) & ((column % tok_dev + 1).astype(F32) == want)
        )

    one = pick(row // 4, lambda r: r % 4, 4)
    two[...] = pick(row // 4 + 2, lambda r: r % 4, 4)
    picker[...] = pick(row // 2, lambda r: r % 2, 2)
    for copy in copies:
        copy.wait()
    first[...] = dot(one, stacked[...]).astype(BF16)


def late_kernel(two, stacked, second):
    second[...] = dot(two[...], stacked[...]).astype(BF16)


def index_kernel(place, ids, gates, row_slot, row_gate, pack, unpack, *, caps, tok_dev):
    slots = ids.shape[1]
    rows = unpack.shape[0]
    experts = rows // 8
    my_dp = place[1]
    owner = ids[...] // tok_dev
    plane = owner % 4
    gate = gates[...]
    rank = jnp.zeros((1, slots), F32)
    for dp in range(4):
        from_owner = owner == iota((experts, slots), 0) * 4 + dp
        count = running_count(from_owner)
        rank += jnp.sum(jnp.where(from_owner, count, 0.0), axis=0, keepdims=True)
    block = iota((8, slots), 0)
    plane_of = jnp.zeros((8, slots), jnp.int32)
    for j, offset in enumerate(OFFSETS):
        plane_of = jnp.where(block == j, (my_dp + offset + 4) % 4, plane_of)
    on_plane = (plane_of == plane) & (block < 4)
    low = on_plane & (rank < 2.5)
    place_low = running_count(low)
    early = low & (place_low < caps[0] + 0.5)
    late = on_plane & ((rank > 2.5) | (place_low > caps[0] + 0.5))
    place_late = running_count(late)
    for j in range(4):
        at = j * sum(caps)
        for group, position, cap in ((early, place_low, caps[0]), (late, place_late, caps[1])):
            row = iota((cap, slots), 0).astype(F32) + 1.0
            hit = (position[j : j + 1, :] == row) & group[j : j + 1, :]
            here = slice(at, at + cap)
            row_slot[here, :] = ones_where(hit)
            row_gate[here, :] = jnp.sum(jnp.where(hit, gate, 0.0), axis=1, keepdims=True)
            at += cap
    row = iota((rows, slots), 0)
    on_row = owner == row // 8 * 4 + my_dp
    own = row_slot[: sum(caps), :]
    for part in range(2):
        arrived = ones_where(on_row & (rank == (row % 8 // 4 + 2 * part + 1).astype(F32)))
        pack[:, part * rows : (part + 1) * rows] = dot(own, arrived, 1, 1).astype(BF16)
    leaving = ones_where(on_row & (rank == (row % 8 // 2 + 1).astype(F32)))
    unpack[...] = dot(leaving, own, 1, 1).astype(BF16)


def count_kernel(everyone, picker, chosen, most, *, tok_dev):
    chosen[...] = picker[...].T
    most[...] = jnp.broadcast_to(fullest(everyone, tok_dev), most.shape).astype(jnp.int32)


def early_kernel(pack, landed, *outs):
    cap = outs[0].shape[0]
    rows, half = landed.shape
    matrix = pack[:cap, :rows]
    quarter = iota(matrix.shape, 1) % 4
    for q in range(4):
        outs[q // 2][:, q % 2 * half : (q % 2 + 1) * half] = dot(
            keep(quarter == q, matrix), landed[...]
        ).astype(BF16)


def pack_kernel(pack, landed_a, landed_b, *refs):
    outs = refs[-2:]
    cap = outs[0].shape[0]
    rows, half = landed_a.shape
    early = pack.shape[0] - cap
    quarter = iota((cap, rows), 1) % 4
    for q in range(4):
        one = dot(keep(quarter == q, pack[early:, :rows]), landed_a[...])
        two = dot(keep(quarter == q, pack[early:, rows:]), landed_b[...])
        outs[q // 2][:, q % 2 * half : (q % 2 + 1) * half] = (one + two).astype(BF16)


def mixed(early, late):
    return jnp.concatenate([part for pair in zip(early, late) for part in pair], axis=0)


def grad_rows(w_in, w_out, tok, cot, gate, slot):
    value, slope = gelu_pair(dot(tok, w_in[...]))
    hidden = value.astype(BF16)
    grad_out = dot(cot, w_out[...], 1, 1)
    per_row = jnp.sum(hidden.astype(F32) * grad_out, axis=1, keepdims=True)
    part = jnp.sum(jnp.where(slot > 0, per_row, 0.0), axis=0, keepdims=True)
    return hidden, (grad_out * gate * slope).astype(BF16), part


def cut(ref, first, size, count):
    return jnp.concatenate([ref[j * count + first : j * count + first + size, :] for j in range(4)], axis=0)


def main_kernel(w_in, w_out, row_gate, row_slot, *refs):
    toks, cots, (hidden, grad_pre, part, *pieces) = refs[:4], refs[4:8], refs[8:]
    early = toks[0].shape[0]
    count = row_gate.shape[0] // 4
    tok = jnp.concatenate([part_of[...] for part_of in toks], axis=0)
    cot = jnp.concatenate([part_of[...] for part_of in cots], axis=0)
    gate = cut(row_gate, 0, early, count)
    hidden[...], grad_pre[...], part[...] = grad_rows(
        w_in, w_out, tok, cot, gate, cut(row_slot, 0, early, count)
    )
    shares(w_in, grad_pre[...], early, pieces, slice(0, early))


def shares(w_in, pre, size, pieces, here):
    half = pieces[0].shape[1]
    for side in range(2):
        share = dot(pre, w_in[side * half : (side + 1) * half, :], 1, 1).astype(BF16)
        for j in range(4):
            pieces[2 * j + side][here, :] = share[j * size : (j + 1) * size, :]


def rest_kernel(w_in, w_out, row_gate, row_slot, hid_a, pre_a, part_a, *refs):
    firsts, toks, cots, (hidden, grad_pre, part, *pieces) = refs[:8], refs[8:12], refs[12:16], refs[16:]
    late = toks[0].shape[0]
    count = row_gate.shape[0] // 4
    early = count - late
    tok = jnp.concatenate([part_of[...] for part_of in toks], axis=0)
    cot = jnp.concatenate([part_of[...] for part_of in cots], axis=0)
    hid_b, pre_b, part_b = grad_rows(
        w_in, w_out, tok, cot, cut(row_gate, early, late, count), cut(row_slot, early, late, count)
    )
    part[...] = part_a[...] + part_b
    for j in range(4):
        for out, one, two in ((hidden, hid_a, hid_b), (grad_pre, pre_a, pre_b)):
            out[j * count : j * count + early, :] = one[j * early : (j + 1) * early, :]
            out[j * count + early : (j + 1) * count, :] = two[j * late : (j + 1) * late, :]
    for out, one in zip(pieces, firsts):
        out[:early, :] = one[...]
    shares(w_in, pre_b, late, pieces, slice(early, count))


def weight_kernel(hidden, row_gate, grad_pre, *refs):
    tok_a, cot_a, tok_b, cot_b = refs[:4], refs[4:8], refs[8:12], refs[12:16]
    grad_in, grad_out = refs[16:]
    gated = (hidden[...].astype(F32) * row_gate[...]).astype(BF16)
    width = grad_in.shape[0]
    step = 512
    for at in range(0, width, step):
        here = slice(at, at + step)
        cot = mixed([near[:, here] for near in cot_a], [near[:, here] for near in cot_b])
        grad_out[:, here] = dot(gated, cot, 0, 0).astype(BF16)
        tok = mixed([near[:, here] for near in tok_a], [near[:, here] for near in tok_b])
        grad_in[here, :] = dot(tok, grad_pre[...], 0, 0).astype(BF16)


def unpack_kernel(unpack, *refs):
    parts, out = refs[:6], refs[6]
    half = out.shape[1]
    matrix = unpack[...]
    side_of = iota(matrix.shape, 0) % 2
    total = jnp.zeros(out.shape, F32)
    for side in range(2):
        summed = sum(part[...].astype(F32) for part in parts[side::2])
        total += dot(keep(side_of == side, matrix), summed.astype(BF16))
    out[...] = total.astype(BF16)


def token_kernel(chosen, landed, out):
    tok_dev, width = out.shape
    half = width // 2
    for side in range(2):
        out[:, side * half : (side + 1) * half] = dot(
            chosen[side * tok_dev : (side + 1) * tok_dev, :], landed[...]
        ).astype(BF16)


def fullest(ids, tok_dev):
    experts, slots = ids.shape
    batch, side = 8, 16
    rows = batch * side
    digit = iota((rows, slots), 0) % side
    same = iota((rows, rows), 0) // side == iota((rows, rows), 1) // side
    column = iota((rows, rows), 0)
    target = iota((rows, rows), 1)
    fold = ones_where((column // side == target // 4) & (column % 4 == target % 4))
    best = jnp.zeros((8, rows), F32)
    for at in range(0, experts, batch):
        owner = jnp.concatenate(
            [jnp.broadcast_to(ids[e : e + 1, :] // tok_dev, (side, slots)) for e in range(at, at + batch)], axis=0
        )
        count = dot(ones_where(owner // side == digit), ones_where(owner % side == digit), 1, 1)
        low = jnp.sum(jnp.where(same, jnp.minimum(count, 2.0), 0.0), axis=0, keepdims=True)
        high = jnp.sum(jnp.where(same, jnp.maximum(count - 2.0, 0.0), 0.0), axis=0, keepdims=True)
        low = dot(jnp.broadcast_to(low, (8, rows)).astype(BF16), fold)
        high = dot(jnp.broadcast_to(high, (8, rows)).astype(BF16), fold)
        best = jnp.maximum(best, high + jnp.maximum(low - SMALL[0], 0.0))
    return jnp.max(best, axis=1, keepdims=True)


def shift(array, step):
    return lax.ppermute(array, "dp", [(d, (d + step) % 4) for d in range(4)])


def add(one, two):
    return (one.astype(F32) + two.astype(F32)).astype(BF16)


def exchange(array):
    return lax.all_to_all(array, "expert", split_axis=0, concat_axis=0, tiled=True)


def path(caps, place, everyone, my_ids, gate, w_in, w_out, picker, first, second):
    width, units = w_in.shape
    rows, half = first.shape
    slots = my_ids.shape[1]
    tok_dev = picker.shape[1] // 2
    early, late = caps
    count = early + late
    landed_a = exchange(first)
    row_slot, row_gate, pack, unpack = call(
        functools.partial(index_kernel, caps=caps, tok_dev=tok_dev),
        [
            shape_of(4 * count, slots),
            shape_of(4 * count, 1, dtype=F32),
            shape_of(count, 2 * rows),
            shape_of(rows, count),
        ],
        place, my_ids, gate, smem=1, flops=4 * count * rows * slots,
    )
    tok, cot = call(early_kernel, [shape_of(early, width)] * 2, pack, landed_a, flops=LONG)
    landed_b = exchange(second)
    left_tok, right_cot = shift(tok, 1), shift(cot, -1)
    left_cot, right_tok = shift(cot, 1), shift(tok, -1)
    chosen, most = call(
        functools.partial(count_kernel, tok_dev=tok_dev),
        [shape_of(2 * tok_dev, rows), shape_of(8, 128, dtype=jnp.int32)], everyone, picker, flops=LONG // 3,
    )
    left_tok, chosen = lax.optimization_barrier((left_tok, chosen))
    right_cot, most = lax.optimization_barrier((right_cot, most))
    toks_a = (tok, left_tok, right_tok, shift(left_tok, 1))
    cots_a = (cot, left_cot, right_cot, shift(right_cot, -1))
    tok, cot = call(
        pack_kernel, [shape_of(late, width)] * 2, pack, landed_a, landed_b, left_tok, right_cot, far=2, flops=LONG
    )
    left_tok, right_cot = shift(tok, 1), shift(cot, -1)
    left_cot, right_tok = shift(cot, 1), shift(tok, -1)
    toks_b = (tok, left_tok, right_tok, shift(left_tok, 1))
    cots_b = (cot, left_cot, right_cot, shift(right_cot, -1))
    product = 2 * 4 * count * width * units
    piece = shape_of(count, half)
    gate_sum = shape_of(1, slots, dtype=F32)
    main = call(
        main_kernel, [shape_of(4 * early, units)] * 2 + [gate_sum] + [shape_of(early, half)] * 8,
        w_in, w_out, row_gate, row_slot, *toks_a, *cots_a, flops=LONG, mib=24,
    )
    hidden, grad_pre, part, own0, own1, left0, left1, right0, right1, far0, far1 = call(
        rest_kernel, [shape_of(4 * count, units)] * 2 + [gate_sum] + [piece] * 8,
        w_in, w_out, row_gate, row_slot, *main, *toks_b, *cots_b, flops=product,
    )
    far0, far1 = shift(far0, 1), shift(far1, -1)
    right1, left0 = shift(right1, 1), shift(left0, -1)
    right0, left1 = shift(add(right0, far0), 1), shift(add(left1, far1), -1)
    back = call(
        unpack_kernel, [shape_of(rows, half)], unpack, own0, own1, left0, left1, right0, right1,
        flops=4 * count * rows * half,
    )[0]
    merged = exchange(back)
    grad_gates = (part + shift(part, 2)) + (shift(part, 1) + shift(part, -1))
    grad_w_in, grad_w_out = call(
        weight_kernel,
        [shape_of(width, units), shape_of(units, width)],
        hidden, row_gate, grad_pre, *toks_a, *cots_a, *toks_b, *cots_b, flops=2 * product,
    )
    grad_tokens = call(token_kernel, [shape_of(tok_dev, width)], chosen, merged, flops=2 * tok_dev * rows * width)[0]
    return (grad_tokens, grad_w_in[None], grad_w_out[None], grad_gates), most


def body(tokens, cotangent, w_in, w_out, expert_tokens, gate_weights):
    tok_dev, width = tokens.shape
    experts, slots = expert_tokens.shape
    expert_idx = lax.axis_index("expert")
    dp_idx = lax.axis_index("dp")
    place = jnp.stack([expert_idx * 4 + dp_idx, dp_idx]).astype(jnp.int32)
    rows = experts * 8
    first, two, picker, stacked = call(
        send_kernel,
        [
            shape_of(rows, width // 2),
            shape_of(rows, 4 * tok_dev),
            shape_of(rows, 2 * tok_dev),
            shape_of(4 * tok_dev, width // 2),
        ],
        place, expert_tokens, tokens, cotangent, smem=1, far=2,
        flops=2 * rows * tok_dev * width * 4,
        scratch=[pltpu.SemaphoreType.DMA((4,))], mib=56,
    )
    second = call(late_kernel, [shape_of(rows, width // 2)], two, stacked, flops=2 * rows * rows * width)[0]
    my_ids = lax.dynamic_slice_in_dim(expert_tokens, expert_idx, 1, 0)
    args = (place, expert_tokens, my_ids, gate_weights, w_in[0], w_out[0], picker, first, second)
    outs, most = path(SMALL, *args)
    state = lax.while_loop(
        lambda state: state[0] > SMALL[1],
        lambda state: (jnp.zeros((), jnp.int32), *path((2 * experts, 2 * experts), *args)[0]),
        (most[0, 0], *outs),
    )
    return state[1:]


def solution(mesh):
    placed = (
        P(("expert", "dp"), None),
        P(("expert", "dp"), None),
        P("expert", None, "dp"),
        P("expert", "dp", None),
        P(),
        P("expert", None),
    )
    return jax.shard_map(
        body,
        mesh=mesh,
        in_specs=placed,
        out_specs=(
            P(("expert", "dp"), None),
            P("expert", None, "dp"),
            P("expert", "dp", None),
            P("expert", None),
        ),
        check_vma=False,
    )
```

```python
import functools

import jax
import jax.numpy as jnp
from jax import lax
from jax.experimental import pallas as pl
from jax.experimental.pallas import tpu as pltpu
from jax.sharding import PartitionSpec as P

GELU_SCALE = 0.7978845608028654
GELU_CUBIC = 0.044715
MOST = 4
BF16 = jnp.bfloat16
F32 = jnp.float32
VMEM = pl.BlockSpec(memory_space=pltpu.VMEM)
SMEM = pl.BlockSpec(memory_space=pltpu.SMEM)
HBM = pl.BlockSpec(memory_space=pltpu.HBM)
OFFSETS = (0, -1, 1, 2)
SMALL = (112, 48)
LONG = 3 * 10**10


def gelu_pair(pre_act):
    inner_arg = GELU_SCALE * (pre_act + GELU_CUBIC * pre_act * pre_act * pre_act)
    tanh_val = jnp.tanh(inner_arg)
    gelu_value = 0.5 * pre_act * (1.0 + tanh_val)
    gelu_slope = 0.5 * (1.0 + tanh_val) + 0.5 * pre_act * (
        1.0 - tanh_val * tanh_val
    ) * GELU_SCALE * (1.0 + 3.0 * GELU_CUBIC * pre_act * pre_act)
    return (gelu_value, gelu_slope)


def dot(a, b, da=1, db=0):
    return lax.dot_general(a, b, (((da,), (db,)), ((), ())), preferred_element_type=F32)


def iota(shape, dim):
    return lax.broadcasted_iota(jnp.int32, shape, dim)


def ones_where(mask):
    return jnp.where(mask, 1.0, 0.0).astype(BF16)


def keep(mask, array):
    return jnp.where(mask, array, jnp.zeros_like(array))


def call(kernel, outs, *args, flops=0, smem=0, far=0, scratch=(), mib=16):
    moved = sum(a.size * a.dtype.itemsize for a in (*args, *outs))
    return pl.pallas_call(
        kernel,
        out_shape=tuple(outs),
        in_specs=[SMEM] * smem + [VMEM] * (len(args) - smem - far) + [HBM] * far,
        out_specs=tuple(VMEM for _ in outs),
        scratch_shapes=list(scratch),
        compiler_params=pltpu.CompilerParams(vmem_limit_bytes=mib * 1024 * 1024),
        cost_estimate=pl.CostEstimate(flops=flops, bytes_accessed=moved, transcendentals=0),
    )(*args)


def shape_of(*dims, dtype=BF16):
    return jax.ShapeDtypeStruct(dims, dtype)


def running_count(mask):
    width = mask.shape[1]
    upper = ones_where(iota((width, width), 0) <= iota((width, width), 1))
    return dot(ones_where(mask), upper)


def send_kernel(place, ids, tokens, cotangent, first, two, picker, stacked, sems):
    experts, _ = ids.shape
    tok_dev, width = tokens.shape
    half = width // 2
    rows = experts * 8
    copies = []
    for q in range(4):
        source = (tokens, cotangent)[q // 2]
        copies.append(
            pltpu.make_async_copy(
                source.at[:, pl.ds(q % 2 * half, half)],
                stacked.at[pl.ds(q * tok_dev, tok_dev), :],
                sems.at[q],
            )
        )
        copies[-1].start()
    id_all = ids[...]
    owner = id_all // tok_dev
    local = id_all - owner * tok_dev
    mine = owner == place[0]
    rank = running_count(mine)
    lane = iota((experts, 128), 1)
    wanted = jnp.zeros((experts, 128), F32)
    for level in range(MOST):
        hit = mine & (rank == level + 1.0)
        found = jnp.sum(jnp.where(hit, local + 1, 0).astype(F32), axis=1, keepdims=True)
        wanted = jnp.where(lane == level, found, wanted)
    spread = ones_where(iota((rows, experts), 0) // 8 == iota((rows, experts), 1))
    by_row = dot(spread, wanted.astype(BF16))
    row = iota((rows, 128), 0) % 8
    lanes = iota((rows, 128), 1)

    def pick(level, part, parts):
        want = jnp.sum(jnp.where(level == lanes, by_row, 0.0), axis=1, keepdims=True)
        column = iota((rows, parts * tok_dev), 1)
        here = iota((rows, parts * tok_dev), 0) % 8
        return ones_where(
            (column // tok_dev == part(here)) & ((column % tok_dev + 1).astype(F32) == want)
        )

    one = pick(row // 4, lambda r: r % 4, 4)
    two[...] = pick(row // 4 + 2, lambda r: r % 4, 4)
    picker[...] = pick(row // 2, lambda r: r % 2, 2)
    for copy in copies:
        copy.wait()
    first[...] = dot(one, stacked[...]).astype(BF16)


def late_kernel(two, stacked, second):
    second[...] = dot(two[...], stacked[...]).astype(BF16)


def index_kernel(place, ids, gates, row_slot, row_gate, pack, unpack, *, caps, tok_dev):
    slots = ids.shape[1]
    rows = unpack.shape[0]
    experts = rows // 8
    my_dp = place[1]
    owner = ids[...] // tok_dev
    plane = owner % 4
    gate = gates[...]
    rank = jnp.zeros((1, slots), F32)
    for dp in range(4):
        from_owner = owner == iota((experts, slots), 0) * 4 + dp
        count = running_count(from_owner)
        rank += jnp.sum(jnp.where(from_owner, count, 0.0), axis=0, keepdims=True)
    block = iota((8, slots), 0)
    plane_of = jnp.zeros((8, slots), jnp.int32)
    for j, offset in enumerate(OFFSETS):
        plane_of = jnp.where(block == j, (my_dp + offset + 4) % 4, plane_of)
    on_plane = (plane_of == plane) & (block < 4)
    low = on_plane & (rank < 2.5)
    place_low = running_count(low)
    early = low & (place_low < caps[0] + 0.5)
    late = on_plane & ((rank > 2.5) | (place_low > caps[0] + 0.5))
    place_late = running_count(late)
    for j in range(4):
        at = j * sum(caps)
        for group, position, cap in ((early, place_low, caps[0]), (late, place_late, caps[1])):
            row = iota((cap, slots), 0).astype(F32) + 1.0
            hit = (position[j : j + 1, :] == row) & group[j : j + 1, :]
            here = slice(at, at + cap)
            row_slot[here, :] = ones_where(hit)
            row_gate[here, :] = jnp.sum(jnp.where(hit, gate, 0.0), axis=1, keepdims=True)
            at += cap
    row = iota((rows, slots), 0)
    on_row = owner == row // 8 * 4 + my_dp
    own = row_slot[: sum(caps), :]
    for part in range(2):
        arrived = ones_where(on_row & (rank == (row % 8 // 4 + 2 * part + 1).astype(F32)))
        pack[:, part * rows : (part + 1) * rows] = dot(own, arrived, 1, 1).astype(BF16)
    leaving = ones_where(on_row & (rank == (row % 8 // 2 + 1).astype(F32)))
    unpack[...] = dot(leaving, own, 1, 1).astype(BF16)


def count_kernel(everyone, picker, chosen, most, *, tok_dev):
    chosen[...] = picker[...].T
    most[...] = jnp.broadcast_to(fullest(everyone, tok_dev), most.shape).astype(jnp.int32)


def by_quarter(matrix):
    quarter = iota(matrix.shape, 1) % 4
    return jnp.concatenate([keep(quarter == q, matrix) for q in range(4)], axis=0)


def early_kernel(pack, landed, *outs):
    cap = outs[0].shape[0]
    rows, half = landed.shape
    matrix = pack[:cap, :rows]
    found = dot(by_quarter(matrix), landed[...]).astype(BF16)
    for q in range(4):
        outs[q // 2][:, q % 2 * half : (q % 2 + 1) * half] = found[q * cap : (q + 1) * cap, :]


def pack_kernel(pack, landed_a, landed_b, *refs):
    outs = refs[-2:]
    cap = outs[0].shape[0]
    rows, half = landed_a.shape
    early = pack.shape[0] - cap
    found = dot(by_quarter(pack[early:, :rows]), landed_a[...])
    found = (found + dot(by_quarter(pack[early:, rows:]), landed_b[...])).astype(BF16)
    for q in range(4):
        outs[q // 2][:, q % 2 * half : (q % 2 + 1) * half] = found[q * cap : (q + 1) * cap, :]


def mixed(early, late):
    return jnp.concatenate([part for pair in zip(early, late) for part in pair], axis=0)


def grad_rows(w_in, w_out, tok, cot, gate, slot):
    value, slope = gelu_pair(dot(tok, w_in[...]))
    hidden = value.astype(BF16)
    grad_out = dot(cot, w_out[...], 1, 1)
    per_row = jnp.sum(hidden.astype(F32) * grad_out, axis=1, keepdims=True)
    part = jnp.sum(jnp.where(slot > 0, per_row, 0.0), axis=0, keepdims=True)
    return hidden, (grad_out * gate * slope).astype(BF16), part


def cut(ref, first, size, count):
    return jnp.concatenate([ref[j * count + first : j * count + first + size, :] for j in range(4)], axis=0)


def main_kernel(w_in, w_out, row_gate, row_slot, *refs):
    toks, cots, (hidden, grad_pre, part, *pieces) = refs[:4], refs[4:8], refs[8:]
    early = toks[0].shape[0]
    count = row_gate.shape[0] // 4
    tok = jnp.concatenate([part_of[...] for part_of in toks], axis=0)
    cot = jnp.concatenate([part_of[...] for part_of in cots], axis=0)
    gate = cut(row_gate, 0, early, count)
    hidden[...], grad_pre[...], part[...] = grad_rows(
        w_in, w_out, tok, cot, gate, cut(row_slot, 0, early, count)
    )
    shares(w_in, grad_pre[...], early, pieces, slice(0, early))


def shares(w_in, pre, size, pieces, here):
    half = pieces[0].shape[1]
    for side in range(2):
        share = dot(pre, w_in[side * half : (side + 1) * half, :], 1, 1).astype(BF16)
        for j in range(4):
            pieces[2 * j + side][here, :] = share[j * size : (j + 1) * size, :]


def rest_kernel(w_in, w_out, row_gate, row_slot, hid_a, pre_a, part_a, *refs):
    firsts, toks, cots, (hidden, grad_pre, part, *pieces) = refs[:8], refs[8:12], refs[12:16], refs[16:]
    late = toks[0].shape[0]
    count = row_gate.shape[0] // 4
    early = count - late
    tok = jnp.concatenate([part_of[...] for part_of in toks], axis=0)
    cot = jnp.concatenate([part_of[...] for part_of in cots], axis=0)
    hid_b, pre_b, part_b = grad_rows(
        w_in, w_out, tok, cot, cut(row_gate, early, late, count), cut(row_slot, early, late, count)
    )
    part[...] = part_a[...] + part_b
    for j in range(4):
        for out, one, two in ((hidden, hid_a, hid_b), (grad_pre, pre_a, pre_b)):
            out[j * count : j * count + early, :] = one[j * early : (j + 1) * early, :]
            out[j * count + early : (j + 1) * count, :] = two[j * late : (j + 1) * late, :]
    for out, one in zip(pieces, firsts):
        out[:early, :] = one[...]
    shares(w_in, pre_b, late, pieces, slice(early, count))


def weight_kernel(hidden, row_gate, grad_pre, *refs):
    tok_a, cot_a, tok_b, cot_b = refs[:4], refs[4:8], refs[8:12], refs[12:16]
    grad_in, grad_out = refs[16:]
    gated = (hidden[...].astype(F32) * row_gate[...]).astype(BF16)
    width = grad_in.shape[0]
    step = 512
    for at in range(0, width, step):
        here = slice(at, at + step)
        cot = mixed([near[:, here] for near in cot_a], [near[:, here] for near in cot_b])
        grad_out[:, here] = dot(gated, cot, 0, 0).astype(BF16)
        tok = mixed([near[:, here] for near in tok_a], [near[:, here] for near in tok_b])
        grad_in[here, :] = dot(tok, grad_pre[...], 0, 0).astype(BF16)


def unpack_kernel(unpack, *refs):
    parts, out = refs[:6], refs[6]
    half = out.shape[1]
    matrix = unpack[...]
    side_of = iota(matrix.shape, 0) % 2
    total = jnp.zeros(out.shape, F32)
    for side in range(2):
        summed = sum(part[...].astype(F32) for part in parts[side::2])
        total += dot(keep(side_of == side, matrix), summed.astype(BF16))
    out[...] = total.astype(BF16)


def token_kernel(chosen, landed, out):
    tok_dev, width = out.shape
    half = width // 2
    found = dot(chosen[...], landed[...]).astype(BF16)
    for side in range(2):
        out[:, side * half : (side + 1) * half] = found[side * tok_dev : (side + 1) * tok_dev, :]


def fullest(ids, tok_dev):
    experts, slots = ids.shape
    batch, side = 8, 16
    rows = batch * side
    digit = iota((rows, slots), 0) % side
    same = iota((rows, rows), 0) // side == iota((rows, rows), 1) // side
    column = iota((rows, rows), 0)
    target = iota((rows, rows), 1)
    fold = ones_where((column // side == target // 4) & (column % 4 == target % 4))
    best = jnp.zeros((8, rows), F32)
    for at in range(0, experts, batch):
        owner = jnp.concatenate(
            [jnp.broadcast_to(ids[e : e + 1, :] // tok_dev, (side, slots)) for e in range(at, at + batch)], axis=0
        )
        count = dot(ones_where(owner // side == digit), ones_where(owner % side == digit), 1, 1)
        low = jnp.sum(jnp.where(same, jnp.minimum(count, 2.0), 0.0), axis=0, keepdims=True)
        high = jnp.sum(jnp.where(same, jnp.maximum(count - 2.0, 0.0), 0.0), axis=0, keepdims=True)
        low = dot(jnp.broadcast_to(low, (8, rows)).astype(BF16), fold)
        high = dot(jnp.broadcast_to(high, (8, rows)).astype(BF16), fold)
        best = jnp.maximum(best, high + jnp.maximum(low - SMALL[0], 0.0))
    return jnp.max(best, axis=1, keepdims=True)


def shift(array, step):
    return lax.ppermute(array, "dp", [(d, (d + step) % 4) for d in range(4)])


def add(one, two):
    return (one.astype(F32) + two.astype(F32)).astype(BF16)


def exchange(array):
    return lax.all_to_all(array, "expert", split_axis=0, concat_axis=0, tiled=True)


def path(caps, place, everyone, my_ids, gate, w_in, w_out, picker, first, second):
    width, units = w_in.shape
    rows, half = first.shape
    slots = my_ids.shape[1]
    tok_dev = picker.shape[1] // 2
    early, late = caps
    count = early + late
    landed_a = exchange(first)
    row_slot, row_gate, pack, unpack = call(
        functools.partial(index_kernel, caps=caps, tok_dev=tok_dev),
        [
            shape_of(4 * count, slots),
            shape_of(4 * count, 1, dtype=F32),
            shape_of(count, 2 * rows),
            shape_of(rows, count),
        ],
        place, my_ids, gate, smem=1, flops=4 * count * rows * slots,
    )
    tok, cot = call(early_kernel, [shape_of(early, width)] * 2, pack, landed_a, flops=LONG)
    landed_b = exchange(second)
    left_tok, right_cot = shift(tok, 1), shift(cot, -1)
    left_cot, right_tok = shift(cot, 1), shift(tok, -1)
    chosen, most = call(
        functools.partial(count_kernel, tok_dev=tok_dev),
        [shape_of(2 * tok_dev, rows), shape_of(8, 128, dtype=jnp.int32)], everyone, picker, flops=LONG // 3,
    )
    left_tok, chosen = lax.optimization_barrier((left_tok, chosen))
    right_cot, most = lax.optimization_barrier((right_cot, most))
    toks_a = (tok, left_tok, right_tok, shift(left_tok, 1))
    cots_a = (cot, left_cot, right_cot, shift(right_cot, -1))
    tok, cot = call(
        pack_kernel, [shape_of(late, width)] * 2, pack, landed_a, landed_b, left_tok, right_cot, far=2, flops=LONG
    )
    left_tok, right_cot = shift(tok, 1), shift(cot, -1)
    left_cot, right_tok = shift(cot, 1), shift(tok, -1)
    toks_b = (tok, left_tok, right_tok, shift(left_tok, 1))
    cots_b = (cot, left_cot, right_cot, shift(right_cot, -1))
    product = 2 * 4 * count * width * units
    piece = shape_of(count, half)
    gate_sum = shape_of(1, slots, dtype=F32)
    main = call(
        main_kernel, [shape_of(4 * early, units)] * 2 + [gate_sum] + [shape_of(early, half)] * 8,
        w_in, w_out, row_gate, row_slot, *toks_a, *cots_a, flops=LONG, mib=24,
    )
    hidden, grad_pre, part, own0, own1, left0, left1, right0, right1, far0, far1 = call(
        rest_kernel, [shape_of(4 * count, units)] * 2 + [gate_sum] + [piece] * 8,
        w_in, w_out, row_gate, row_slot, *main, *toks_b, *cots_b, flops=product,
    )
    far0, far1 = shift(far0, 1), shift(far1, -1)
    right1, left0 = shift(right1, 1), shift(left0, -1)
    right0, left1 = shift(add(right0, far0), 1), shift(add(left1, far1), -1)
    back = call(
        unpack_kernel, [shape_of(rows, half)], unpack, own0, own1, left0, left1, right0, right1,
        flops=4 * count * rows * half,
    )[0]
    merged = exchange(back)
    grad_gates = (part + shift(part, 2)) + (shift(part, 1) + shift(part, -1))
    grad_w_in, grad_w_out = call(
        weight_kernel,
        [shape_of(width, units), shape_of(units, width)],
        hidden, row_gate, grad_pre, *toks_a, *cots_a, *toks_b, *cots_b, flops=2 * product,
    )
    grad_tokens = call(token_kernel, [shape_of(tok_dev, width)], chosen, merged, flops=2 * tok_dev * rows * width)[0]
    return (grad_tokens, grad_w_in[None], grad_w_out[None], grad_gates), most


def body(tokens, cotangent, w_in, w_out, expert_tokens, gate_weights):
    tok_dev, width = tokens.shape
    experts, slots = expert_tokens.shape
    expert_idx = lax.axis_index("expert")
    dp_idx = lax.axis_index("dp")
    place = jnp.stack([expert_idx * 4 + dp_idx, dp_idx]).astype(jnp.int32)
    rows = experts * 8
    first, two, picker, stacked = call(
        send_kernel,
        [
            shape_of(rows, width // 2),
            shape_of(rows, 4 * tok_dev),
            shape_of(rows, 2 * tok_dev),
            shape_of(4 * tok_dev, width // 2),
        ],
        place, expert_tokens, tokens, cotangent, smem=1, far=2,
        flops=2 * rows * tok_dev * width * 4,
        scratch=[pltpu.SemaphoreType.DMA((4,))], mib=56,
    )
    second = call(late_kernel, [shape_of(rows, width // 2)], two, stacked, flops=2 * rows * rows * width)[0]
    my_ids = lax.dynamic_slice_in_dim(expert_tokens, expert_idx, 1, 0)
    args = (place, expert_tokens, my_ids, gate_weights, w_in[0], w_out[0], picker, first, second)
    outs, most = path(SMALL, *args)
    state = lax.while_loop(
        lambda state: state[0] > SMALL[1],
        lambda state: (jnp.zeros((), jnp.int32), *path((2 * experts, 2 * experts), *args)[0]),
        (most[0, 0], *outs),
    )
    return state[1:]


def solution(mesh):
    placed = (
        P(("expert", "dp"), None),
        P(("expert", "dp"), None),
        P("expert", None, "dp"),
        P("expert", "dp", None),
        P(),
        P("expert", None),
    )
    return jax.shard_map(
        body,
        mesh=mesh,
        in_specs=placed,
        out_specs=(
            P(("expert", "dp"), None),
            P("expert", None, "dp"),
            P("expert", "dp", None),
            P("expert", None),
        ),
        check_vma=False,
    )
```
